256 devices in a mesh: region: 32 (over z, x), cols: 8 (over y, core).
Axes of the slice: x: 4, y: 4, z: 8, core: 2. Of those that a mesh axis runs over, the one named last changes fastest.
Arguments:
- innovations: float32 [32, 262144], P('cols', 'region'), may hold values from -6 to 6
- coords: float32 [3, 262144], P(None, 'region'), may hold values from -1 to 1, as said below
- background_std: float32 [262144], P('region'), may hold values from 0.3 to 1.2
- obs_variance: float32 [262144], P('region'), may hold values from 0.25 to 1
- block_count: int32 [1024], P('region'), may hold values from 128 to 256, as said below
- pair_list: int32 [2, 24576], P(None, ('region', 'cols')), may hold values from 0 to 54, as said below
- pair_count: int32 [256], P(('region', 'cols')), may hold values from 4 to 96, as said below
Outputs:
- solution_field: float32 [32, 262144], P('cols', 'region')
- residual: float32 [32, 262144], P('cols', 'region')
The draws below stay inside these ranges and needn't reach their ends.
Inputs may be any that keep to these rules, and one draw needn't show every extreme that they name: `coords`: every column is a unit vector. `block_count`: the first block of every region holds 256 live observations. `pair_list`: live entries of a device come first in its 96 slots; row 0 names a block whose index within the region lies among the device's own 32 // (devices on cols) blocks (the device at cols position c owns blocks c * that many onward), row 1 is at least row 0 and at most row 23, and the partner block exists; no unordered pair appears twice; dead slots hold 0. `pair_count`: some device has all 96 slots live.
All inputs are finite; a program needn't handle non-finite values.
Results may differ from the reference program's by a relative error of at most 0.0003.
Values sent between devices are 32-bit elements; how exact they have to be, the bound alone decides.
No kernel may reach another device: no remote copies, remote signals or barrier semaphores. Data moves between devices by JAX's collectives and lax.ppermute only.
A program may use at most 64 MiB of HBM per device.

```python
import math
import jax
import jax.numpy as jnp
from jax import lax

BLOCK = 256
NRHS = 32
NB_REG = 32
KMAX = 23
ITERS = 2
NBLK = 1024
NOBS = 262144
PAIRS_DEV = 96
NPAIRS = 24576
N_COLS = 8


SUPPORT = 1000.0 / 6371.0


def pair_layout(key):
    reach_key = jax.random.fold_in(key, 21)
    full_key = jax.random.fold_in(key, 22)
    device_total = NPAIRS // PAIRS_DEV
    per_device = PAIRS_DEV // (KMAX + 1)
    col_total = NB_REG // per_device
    reach_max = jax.random.randint(reach_key, (device_total, per_device), 0, KMAX + 1)
    full_device = jax.random.randint(full_key, (), 0, col_total)
    device_ids = jnp.arange(device_total)
    reach_max = jnp.where((device_ids == full_device)[:, None], KMAX, reach_max)
    own_blocks = (device_ids % col_total)[:, None] * per_device + jnp.arange(per_device)[None, :]
    region_ids = device_ids // col_total
    offsets = jnp.arange(KMAX + 1)
    far_blocks = own_blocks[:, :, None] + offsets[None, None, :]
    usable = (offsets[None, None, :] <= reach_max[:, :, None]) & ((region_ids * NB_REG)[:, None, None] + far_blocks < NBLK)
    near_flat = jnp.broadcast_to(own_blocks[:, :, None], far_blocks.shape).reshape(device_total, PAIRS_DEV)
    far_flat = far_blocks.reshape(device_total, PAIRS_DEV)
    usable_flat = usable.reshape(device_total, PAIRS_DEV).astype(jnp.int32)
    slot_ids = jnp.arange(PAIRS_DEV)[None, :]
    order_keys = jnp.where(usable_flat > 0, slot_ids, slot_ids + PAIRS_DEV)
    slot_order = jnp.argsort(order_keys, axis=1)
    near_sorted = jnp.take_along_axis(near_flat * usable_flat, slot_order, axis=1)
    far_sorted = jnp.take_along_axis(far_flat * usable_flat, slot_order, axis=1)
    counts = jnp.sum(usable_flat, axis=1).astype(jnp.int32)
    pairs = jnp.stack([near_sorted.reshape(-1), far_sorted.reshape(-1)]).astype(jnp.int32)
    return (pairs, counts)


def draw_pair_list(key, part):
    return pair_layout(key)[0]


def draw_pair_count(key, part):
    return pair_layout(key)[1]


def draw_block_count(key, part):
    key = jax.random.fold_in(key, 5)
    counts = jax.random.randint(key, (NBLK,), BLOCK // 2, BLOCK + 1)
    return jnp.where(jnp.arange(NBLK) % NB_REG == 0, BLOCK, counts).astype(jnp.int32)


def draw_coords(key, part):
    key = jax.random.fold_in(key, 11)
    blocks = (jnp.arange(NOBS) // BLOCK).astype(jnp.float32)
    theta = blocks * (0.8 * SUPPORT / KMAX)
    height = -0.9 + 1.8 * (blocks + 0.5) / NBLK
    cycle = jnp.sqrt(1.0 - height * height)
    radius = 0.5 * SUPPORT
    shifts = jax.random.uniform(key, (2, NOBS), jnp.float32, -radius, radius)
    along = shifts[0]
    across = shifts[1]
    point_x = cycle * jnp.cos(theta) - along * jnp.sin(theta) - across * height * jnp.cos(theta)
    point_y = cycle * jnp.sin(theta) + along * jnp.cos(theta) - across * height * jnp.sin(theta)
    point_z = height + across * cycle
    length = jnp.sqrt(point_x * point_x + point_y * point_y + point_z * point_z)
    return jnp.stack([point_x / length, point_y / length, point_z / length]).astype(jnp.float32)


def shard_levels(key, dims, pieces, smallest, largest):
    gain, own = 1.0, jax.random.fold_in(key, 6)
    for axis_at, shards_of in pieces:
        draws = jnp.exp(jax.random.uniform(jax.random.fold_in(own, axis_at), (shards_of,), jnp.float32, smallest / len(pieces), largest / len(pieces)))
        gain = gain * jnp.repeat(draws, dims[axis_at] // shards_of).reshape([-1 if axis == axis_at else 1 for axis in range(len(dims))])
    return gain


def scatter_about(rng, shape, scale, limit, shards=(), held_as=jnp.bfloat16):
    level = shard_levels(rng, shape, shards, -0.22, 0.18) if shards else 1.0
    entries = jax.random.normal(rng, shape, jnp.float32) * scale * level
    return jnp.minimum(jnp.maximum(entries, -limit), limit).astype(held_as)


def setup_inputs(seed: int = 0) -> dict:
    key_of = jax.random.split(jax.random.key(seed), 8)
    return {
        "innovations": scatter_about(key_of[0], (NRHS, NOBS), 1.0, 6.0, ((0, 8), (1, 32)), jnp.float32),
        "coords": draw_coords(jax.random.fold_in(key_of[7], 71), 0),
        "background_std": jnp.clip(jnp.exp(math.log(1.2) - 1.3862944 * jax.random.uniform(key_of[2], (NOBS,), jnp.float32) ** shard_levels(key_of[2], (NOBS,), ((0, 32),), -0.2, 0.2)), 0.3, 1.2),
        "obs_variance": jnp.clip(jnp.exp(math.log(1.0) - 1.3862944 * jax.random.uniform(key_of[3], (NOBS,), jnp.float32) ** shard_levels(key_of[3], (NOBS,), ((0, 32),), -0.2, 0.2)), 0.25, 1.0),
        "block_count": draw_block_count(jax.random.fold_in(key_of[7], 71), 0),
        "pair_list": draw_pair_list(jax.random.fold_in(key_of[7], 71), 0),
        "pair_count": draw_pair_count(jax.random.fold_in(key_of[7], 71), 0),
    }


SUPPORT = 1000.0 / 6371.0
pair_group = 8

def cov_tiles(coord_blk, spread_blk, vec_blk, left_blocks, right_blocks, weights):
    left_pts = coord_blk[:, left_blocks]
    right_pts = coord_blk[:, right_blocks]
    inner_sum = left_pts[0][:, :, None] * right_pts[0][:, None, :]
    inner_sum = inner_sum + left_pts[1][:, :, None] * right_pts[1][:, None, :]
    inner_sum = inner_sum + left_pts[2][:, :, None] * right_pts[2][:, None, :]
    distance_ratio = jnp.sqrt(jnp.maximum(2.0 - 2.0 * inner_sum, 0.0)) / SUPPORT
    falloff = jnp.maximum(1.0 - distance_ratio, 0.0) ** 4 * (4.0 * distance_ratio + 1.0)
    tile_values = spread_blk[left_blocks][:, :, None] * falloff * spread_blk[right_blocks][:, None, :]
    into_left = jnp.einsum('rgb,gab->rga', vec_blk[:, right_blocks], tile_values, precision=lax.Precision.HIGHEST)
    into_left = into_left * weights[None, :, None]
    mirror = weights * (left_blocks != right_blocks).astype(weights.dtype)
    into_right = jnp.einsum('rga,gab->rgb', vec_blk[:, left_blocks], tile_values, precision=lax.Precision.HIGHEST)
    into_right = into_right * mirror[None, :, None]
    return (into_left, into_right)

def reference(innovations, coords, background_std, obs_variance, block_count, pair_list, pair_count):
    live_mask = (jnp.arange(BLOCK)[None, :] < block_count[:, None]).astype(jnp.float32).reshape(-1)
    spread = background_std * live_mask
    coord_blk = coords.reshape(3, NBLK, BLOCK)
    spread_blk = spread.reshape(NBLK, BLOCK)
    pair_ids = jnp.arange(NPAIRS).astype(jnp.int32)
    device_ids = pair_ids // PAIRS_DEV
    base_block = device_ids // N_COLS * NB_REG
    left_all = (base_block + pair_list[0]).astype(jnp.int32).reshape(-1, pair_group)
    right_all = (base_block + pair_list[1]).astype(jnp.int32).reshape(-1, pair_group)
    weight_all = (pair_ids % PAIRS_DEV < pair_count[device_ids]).astype(jnp.float32).reshape(-1, pair_group)

    def apply_operator(vector):
        vec_blk = vector.reshape(NRHS, NBLK, BLOCK)

        def one_group(totals, members):
            left_blocks, right_blocks, weights = members
            into_left, into_right = cov_tiles(coord_blk, spread_blk, vec_blk, left_blocks, right_blocks, weights)
            totals = totals.at[:, left_blocks].add(into_left).at[:, right_blocks].add(into_right)
            return (totals, None)
        totals, unused = lax.scan(one_group, jnp.zeros_like(vec_blk), (left_all, right_all, weight_all))
        return totals.reshape(NRHS, -1) + obs_variance[None, :] * vector
    solution_field = jnp.zeros_like(innovations)
    residual = innovations
    direction = innovations
    norm_now = lax.optimization_barrier(jnp.sum(residual * residual, axis=1))
    for step_index in range(ITERS):
        image = apply_operator(direction)
        alpha = norm_now / lax.optimization_barrier(jnp.sum(direction * image, axis=1))
        solution_field = solution_field + alpha[:, None] * direction
        residual = residual - alpha[:, None] * image
        norm_next = lax.optimization_barrier(jnp.sum(residual * residual, axis=1))
        direction = residual + (norm_next / norm_now)[:, None] * direction
        norm_now = norm_next
    return (solution_field, residual)
```

```python
import functools

import jax
import jax.numpy as jnp
from jax import lax
from jax.experimental import pallas as pl
from jax.experimental.pallas import tpu as pltpu
from jax.sharding import PartitionSpec as P

BLOCK = 256
KMAX = 23
SUPPORT = 1000.0 / 6371.0

STRETCH = 4.0**0.2
TOP = 5.0 / STRETCH**4
GAMMA = 2.0 * STRETCH**2 / SUPPORT**2
FAR = 2.0**100

ROWS = 32
CHIP = 8 * BLOCK
HALF = 4 * BLOCK
WIDE = CHIP + 128
AXES = ("region", "cols")

bf16 = jnp.bfloat16
f32 = jnp.float32


def dot(a, b):
    return jnp.dot(a, b, preferred_element_type=f32)


def two_parts(x):
    high = x.astype(bf16)
    return high, (x - high.astype(f32)).astype(bf16)


def three_parts(x):
    first = x.astype(bf16).astype(f32)
    rest = x - first
    second = rest.astype(bf16).astype(f32)
    return first, second, (rest - second).astype(bf16).astype(f32)


def vmem(count):
    return [pl.BlockSpec(memory_space=pltpu.VMEM)] * count


def smem(count):
    return [pl.BlockSpec(memory_space=pltpu.SMEM)] * count


def params(mebibytes):
    return pltpu.CompilerParams(vmem_limit_bytes=mebibytes * 1024 * 1024)


def prepare_kernel(
    place, counts, gathered, coords, std, variance, halo, vector, aux
):
    row_at, core = place[0], place[1]
    halo[32:40, :] = jnp.zeros((8, WIDE), f32)
    halo[0:32, CHIP:] = jnp.zeros((32, 128), f32)
    lane = lax.broadcasted_iota(jnp.int32, (1, BLOCK), 1)
    for j in range(8):
        source = j + core * (7 - 2 * j)
        here = slice(j * BLOCK, (j + 1) * BLOCK)
        local = pl.ds(pl.multiple_of(source * BLOCK, BLOCK), BLOCK)
        region = pl.ds(pl.multiple_of((row_at * 8 + source) * BLOCK, BLOCK), BLOCK)
        live = (lane < counts[row_at * 8 + source]).astype(f32)
        spread = std[0:1, region] * live
        values = gathered[:, local]
        vector[:, here] = values
        halo[0:32, here] = values * spread
        halo[32:35, here] = coords[:, region]
        aux[0:1, here] = spread
        aux[1:2, here] = variance[0:1, region]
    sub = lax.broadcasted_iota(jnp.int32, (8, 128), 0)
    col = lax.broadcasted_iota(jnp.int32, (8, 128), 1)
    far = col < 24
    mine = col - lax.div(col, 8) * 8
    ahead = 8 * (lax.div(col, 8) + 1)
    offset = jnp.where(far, ahead + sub - mine, jnp.abs(mine - sub))
    left_up = jnp.where(far, mine, jnp.minimum(mine, sub))
    left_down = jnp.where(far, 7 - sub, 7 - jnp.maximum(mine, sub))
    left = jnp.where(core == 0, left_up, left_down)
    valid = (offset >= 0) & (offset <= KMAX) & (col < 32)
    target = jnp.where(valid, (row_at * 8 + left) * 24 + offset, -7).astype(f32)
    codes = gathered[pl.ds(pl.multiple_of(row_at * 8, 8), 8), CHIP:WIDE]
    hit = jnp.zeros((8, 128), f32)
    for source in (0, 4):
        for i in range(96):
            code = jnp.broadcast_to(codes[source : source + 1, i : i + 1], (8, 128))
            hit = jnp.where(code == target, 1.0, hit)
    halo[32:40, CHIP:] = jnp.where(hit > 0.5, 0.0, FAR)


def prepare(place, counts, gathered, coords, std, variance):
    return pl.pallas_call(
        prepare_kernel,
        out_shape=(
            jax.ShapeDtypeStruct((40, WIDE), f32),
            jax.ShapeDtypeStruct((ROWS, CHIP), f32),
            jax.ShapeDtypeStruct((8, CHIP), f32),
        ),
        in_specs=smem(2) + vmem(4),
        out_specs=vmem(3),
        compiler_params=params(8),
        name="prepare",
    )(place, counts, gathered, coords, std, variance)


def covariance(left, right):
    x = jnp.maximum(dot(left, right), 1e-30)
    z = jnp.maximum(STRETCH - x * lax.rsqrt(x), 0.0)
    z2 = z * z
    return two_parts(z2 * z2 * (TOP - z))


def own_side(own):
    sub = lax.broadcasted_iota(jnp.int32, (8, CHIP), 0)
    points = own[32:40, 0:CHIP]
    side = jnp.where(sub < 3, points * (-GAMMA), jnp.where(sub == 3, GAMMA, 0.0))
    return three_parts(side)


def far_side(points):
    sub = lax.broadcasted_iota(jnp.int32, (8, BLOCK), 0)
    b1, b2, b3 = three_parts(
        jnp.where(sub < 3, points, jnp.where(sub < 5, 1.0, 0.0))
    )
    return jnp.concatenate([b1, b2, b1, b2, b3, b1], 0).T.astype(bf16)


def masks(place, own, halo, offset, spread_out):
    column = 24 if offset == 0 else 8 * (offset - 1)
    flags = jnp.where(
        place[1] == 0, own[32:40, CHIP:WIDE], halo[32:40, CHIP:WIDE]
    )
    for a in range(8):
        spread_out[:, a * BLOCK : (a + 1) * BLOCK] = jnp.broadcast_to(
            flags[:, column + a : column + a + 1], (8, BLOCK)
        )


def tiles_kernel(offset, place, own, halo, before, high, low, total, right, mask):
    a1, a2, a3 = own_side(own)
    right[16:32, :] = jnp.concatenate([a2, a2], 0).astype(bf16)
    right[32:48, :] = jnp.concatenate([a1, a3], 0).astype(bf16)
    masks(place, own, halo, offset, mask)
    if offset == 0:
        total[...] = jnp.zeros_like(total)
    else:
        total[...] = before[...]
    sub = lax.broadcasted_iota(jnp.int32, (8, CHIP), 0)

    def one_block(b, carry):
        rows = pl.ds(pl.multiple_of(b * BLOCK, BLOCK), BLOCK)
        left = far_side(halo[32:40, rows])
        row = jnp.broadcast_to(mask[pl.ds(b, 1), :], (8, CHIP))
        right[0:16, :] = jnp.concatenate(
            [jnp.where(sub == 4, row, a1), a1], 0
        ).astype(bf16)
        uh, ul = two_parts(halo[0:32, rows])
        both = jnp.concatenate([uh, ul], 0)
        for a in range(8):
            here = slice(a * BLOCK, (a + 1) * BLOCK)
            th, tl = covariance(left, right[:, here])
            high[rows, here] = th
            low[rows, here] = tl
            total[:, here] += dot(both, th)
            total[0:32, here] += dot(uh, tl)
        return carry

    lax.fori_loop(0, 4 if offset == 0 else 8, one_block, 0)


def tiles(offset, place, own, halo, before):
    depth = HALF if offset == 0 else CHIP
    return pl.pallas_call(
        functools.partial(tiles_kernel, offset),
        out_shape=(
            pltpu.VMEM((depth, CHIP), bf16),
            pltpu.VMEM((depth, CHIP), bf16),
            jax.ShapeDtypeStruct((2 * ROWS, CHIP), f32),
        ),
        in_specs=smem(1) + vmem(3),
        out_specs=vmem(3),
        scratch_shapes=[pltpu.VMEM((48, CHIP), bf16), pltpu.VMEM((8, CHIP), f32)],
        compiler_params=params(10),
        name=f"tiles{offset}",
    )(place, own, halo, before)


def edge_kernel(place, own, halo, before, high, low, product, right, first, mask, left, total):
    a1, a2, a3 = own_side(own)
    right[0:16, :] = jnp.concatenate([a2, a2], 0).astype(bf16)
    right[16:32, :] = jnp.concatenate([a1, a3], 0).astype(bf16)
    masks(place, own, halo, 3, mask)
    total[...] = before[...]
    sub = lax.broadcasted_iota(jnp.int32, (8, CHIP), 0)

    def one_side(j, carry):
        rows = pl.ds(pl.multiple_of(j * BLOCK, BLOCK), BLOCK)
        left[rows, :] = far_side(halo[32:40, rows])
        row = jnp.broadcast_to(mask[pl.ds(j, 1), :], (8, CHIP))
        first[pl.ds(pl.multiple_of(j * 16, 16), 16), :] = jnp.concatenate(
            [jnp.where(sub == 4, row, a1), a1], 0
        ).astype(bf16)
        return carry

    lax.fori_loop(0, 7, one_side, 0)

    def one_group(g, carry):
        for s in range(7):
            inner = s < 7 - g
            j = jnp.where(inner, g, 7 - g)
            a = s + 1 + jnp.where(inner, g, 0)
            rows = pl.ds(pl.multiple_of(j * BLOCK, BLOCK), BLOCK)
            here = pl.ds(pl.multiple_of(a * BLOCK, BLOCK), BLOCK)
            at = (lax.div(a * (a - 1), 2) + j) * BLOCK
            keep = pl.ds(pl.multiple_of(at, BLOCK), BLOCK)
            side = jnp.concatenate(
                [
                    first[pl.ds(pl.multiple_of(j * 16, 16), 16), here],
                    right[:, here],
                ],
                0,
            )
            th, tl = covariance(left[rows, :], side)
            high[keep, :] = th
            low[keep, :] = tl
            uh, ul = two_parts(halo[0:32, rows])
            total[:, here] += dot(jnp.concatenate([uh, ul], 0), th)
            total[0:32, here] += dot(uh, tl)
        return carry

    lax.fori_loop(0, 4, one_group, 0)
    product[...] = total[0:32, :] + total[32:64, :]


def edge_tiles(place, own, halo, before):
    return pl.pallas_call(
        edge_kernel,
        out_shape=(
            pltpu.VMEM((28 * BLOCK, BLOCK), bf16),
            pltpu.VMEM((28 * BLOCK, BLOCK), bf16),
            jax.ShapeDtypeStruct((ROWS, CHIP), f32),
        ),
        in_specs=smem(1) + vmem(3),
        out_specs=vmem(3),
        scratch_shapes=[
            pltpu.VMEM((32, CHIP), bf16),
            pltpu.VMEM((7 * 16, CHIP), bf16),
            pltpu.VMEM((8, CHIP), f32),
            pltpu.VMEM((CHIP, 48), bf16),
            pltpu.VMEM((2 * ROWS, CHIP), f32),
        ],
        compiler_params=params(10),
        name="tiles3",
    )(place, own, halo, before)


def apply_kernel(depth, vector, high, low, before, total):
    uh, ul = two_parts(vector[:, 0:depth])
    both = jnp.concatenate([uh, ul], 0)
    for n in range(0, CHIP, 512):
        here = slice(n, n + 512)
        pair = dot(both, high[:, here])
        extra = dot(uh, low[:, here])
        total[:, here] = before[:, here] + ((pair[0:32] + pair[32:64]) + extra)


def apply(vector, high, low, before):
    depth = high.shape[0]
    return pl.pallas_call(
        functools.partial(apply_kernel, depth),
        out_shape=jax.ShapeDtypeStruct((ROWS, CHIP), f32),
        in_specs=vmem(4),
        out_specs=vmem(1)[0],
        compiler_params=params(8),
        name="apply",
    )(vector, high, low, before)


def edge_apply_kernel(vector, high, low, before, total):
    uh, ul = two_parts(vector[...])
    both = jnp.concatenate([uh, ul], 0)
    total[:, 0:BLOCK] = before[:, 0:BLOCK]
    for a in range(1, 8):
        rows = slice(a * (a - 1) // 2 * BLOCK, a * (a + 1) // 2 * BLOCK)
        here = slice(a * BLOCK, (a + 1) * BLOCK)
        pair = dot(both[:, 0 : a * BLOCK], high[rows, :])
        extra = dot(uh[:, 0 : a * BLOCK], low[rows, :])
        total[:, here] = before[:, here] + ((pair[0:32] + pair[32:64]) + extra)


def edge_apply(vector, high, low, before):
    return pl.pallas_call(
        edge_apply_kernel,
        out_shape=jax.ShapeDtypeStruct((ROWS, CHIP), f32),
        in_specs=vmem(4),
        out_specs=vmem(1)[0],
        compiler_params=params(8),
        name="apply3",
    )(vector, high, low, before)


def combine_kernel(mine, other, aux, vector, image, scaled):
    for j in range(8):
        here = slice(j * BLOCK, (j + 1) * BLOCK)
        there = slice((7 - j) * BLOCK, (8 - j) * BLOCK)
        spread = aux[0:1, here]
        value = (mine[:, here] + other[:, there]) * spread
        value = value + aux[1:2, here] * vector[:, here]
        image[:, here] = value
        scaled[:, here] = value * spread


def combine(mine, other, aux, vector):
    shape = jax.ShapeDtypeStruct((ROWS, CHIP), f32)
    return pl.pallas_call(
        combine_kernel,
        out_shape=(shape, shape),
        in_specs=vmem(4),
        out_specs=vmem(2),
        compiler_params=params(8),
        name="combine",
    )(mine, other, aux, vector)


def finish_kernel(place, mine, other, aux, vector, image, out):
    core = place[1]
    sums = [jnp.zeros((ROWS, 1), f32) for _ in range(4)]
    for j in range(4):
        here = slice(j * BLOCK, (j + 1) * BLOCK)
        there = slice((7 - j) * BLOCK, (8 - j) * BLOCK)
        last = (mine[:, here] + other[:, there]) * aux[0:1, here]
        last = last + aux[1:2, here] * image[:, here]
        place_at = j + core * (3 - 2 * j)
        out[:, pl.ds(pl.multiple_of(place_at * BLOCK, BLOCK), BLOCK)] = image[:, here]
        out[:, pl.ds(pl.multiple_of(HALF + place_at * BLOCK, BLOCK), BLOCK)] = last
        terms = (
            vector[:, here] * vector[:, here],
            vector[:, here] * image[:, here],
            image[:, here] * image[:, here],
            image[:, here] * last,
        )
        sums = [s + jnp.sum(t, axis=1, keepdims=True) for s, t in zip(sums, terms)]
    lane = lax.broadcasted_iota(jnp.int32, (ROWS, 128), 1)
    packed = jnp.zeros((ROWS, 128), f32)
    for i in range(4):
        packed = jnp.where(lane == i, sums[i], packed)
    out[:, CHIP:] = packed


def finish(place, mine, other, aux, vector, image):
    return pl.pallas_call(
        finish_kernel,
        out_shape=jax.ShapeDtypeStruct((ROWS, WIDE), f32),
        in_specs=smem(1) + vmem(5),
        out_specs=vmem(1)[0],
        compiler_params=params(8),
        name="finish",
    )(place, mine, other, aux, vector, image)


def neighbours(block, step, chips):
    route = [(2 * (m + step), 2 * m) for m in range(chips - step)]
    route += [(2 * m + 1, 2 * (m + step) + 1) for m in range(chips - step)]
    return lax.ppermute(block, AXES, route)


def sibling(block, chips):
    route = [(i, i ^ 1) for i in range(2 * chips)]
    return lax.ppermute(block, AXES, route)


def per_device(
    innovations, coords, background_std, obs_variance, block_count, pair_list, pair_count
):
    chips = lax.axis_size("region") * lax.axis_size("cols") // 2
    column = lax.axis_index("cols")
    place = jnp.stack([column // 2, column % 2]).astype(jnp.int32)

    slots = jnp.arange(128)
    codes = jnp.pad(pair_list[0] * 24 + (pair_list[1] - pair_list[0]), (0, 32))
    codes = jnp.where(slots < pair_count[0], codes, -1).astype(f32)
    rows = innovations.reshape(4, 4, CHIP).transpose(1, 0, 2)
    rows = jnp.concatenate([rows, jnp.broadcast_to(codes, (4, 4, 128))], 2)
    rows = jnp.broadcast_to(rows[:, None], (4, 2, 4, WIDE)).reshape(8, 4, WIDE)
    gathered = lax.all_to_all(rows, "cols", 0, 0, tiled=True).reshape(ROWS, WIDE)

    own, vector, aux = prepare(
        place,
        block_count,
        gathered,
        coords,
        background_std.reshape(1, -1),
        obs_variance.reshape(1, -1),
    )
    halos = [own] + [neighbours(own, step, chips) for step in (1, 2, 3)]
    kept, total = [], jnp.zeros((2 * ROWS, CHIP), f32)
    for offset in range(3):
        high, low, total = tiles(offset, place, own, halos[offset], total)
        kept.append((high, low))
    high, low, product = edge_tiles(place, own, halos[3], total)
    kept.append((high, low))
    image, scaled = combine(product, sibling(product, chips), aux, vector)

    halos = [scaled] + [neighbours(scaled, step, chips) for step in (1, 2, 3)]
    product = jnp.zeros((ROWS, CHIP), f32)
    for offset in range(3):
        product = apply(halos[offset], *kept[offset], product)
    product = edge_apply(halos[3], *kept[3], product)
    sent = finish(place, product, sibling(product, chips), aux, vector, image)

    back = lax.all_to_all(sent.reshape(8, 4, WIDE), "cols", 0, 0, tiled=True)
    first = back[:, :, 0:HALF].transpose(1, 0, 2).reshape(4, -1)
    second = back[:, :, HALF:CHIP].transpose(1, 0, 2).reshape(4, -1)
    sums = jnp.sum(back[:, :, CHIP : CHIP + 4], axis=0)
    regions = lax.axis_size("region")
    sums = lax.all_to_all(
        jnp.broadcast_to(sums.reshape(1, 16), (regions, 16)), "region", 0, 0, tiled=True
    )
    sums = jnp.sum(sums, axis=0).reshape(4, 4)
    bb, bk, kk, kl = (sums[:, i : i + 1] for i in range(4))
    alpha = bb / bk
    norm = alpha * alpha * kk - 2.0 * alpha * bk + bb
    beta = norm / bb
    grown = 1.0 + beta
    energy = grown * grown * bk - 2.0 * alpha * grown * kk + alpha * alpha * kl
    step = norm / energy
    direction = grown * innovations - alpha * first
    field = alpha * innovations + step * direction
    residual = innovations - alpha * first - step * (grown * first - alpha * second)
    return field, residual


def solution(mesh):
    placed = (
        P("cols", "region"),
        P(None, "region"),
        P("region"),
        P("region"),
        P("region"),
        P(None, ("region", "cols")),
        P(("region", "cols")),
    )
    return jax.shard_map(
        per_device,
        mesh=mesh,
        in_specs=placed,
        out_specs=(P("cols", "region"), P("cols", "region")),
        check_vma=False,
    )
```

```python
import functools

import jax
import jax.numpy as jnp
from jax import lax
from jax.experimental import pallas as pl
from jax.experimental.pallas import tpu as pltpu
from jax.sharding import PartitionSpec as P

BLOCK = 256
KMAX = 23
SUPPORT = 1000.0 / 6371.0

STRETCH = 4.0**0.2
TOP = 5.0 / STRETCH**4
GAMMA = 2.0 * STRETCH**2 / SUPPORT**2
FAR = 2.0**100

ROWS = 32
CHIP = 8 * BLOCK
HALF = 4 * BLOCK
WIDE = CHIP + 128
AXES = ("region", "cols")

bf16 = jnp.bfloat16
f32 = jnp.float32


def dot(a, b):
    return jnp.dot(a, b, preferred_element_type=f32)


def two_parts(x):
    high = x.astype(bf16)
    return high, (x - high.astype(f32)).astype(bf16)


def three_parts(x):
    first = x.astype(bf16).astype(f32)
    rest = x - first
    second = rest.astype(bf16).astype(f32)
    return first, second, (rest - second).astype(bf16).astype(f32)


def vmem(count):
    return [pl.BlockSpec(memory_space=pltpu.VMEM)] * count


def smem(count):
    return [pl.BlockSpec(memory_space=pltpu.SMEM)] * count


def hbm(count):
    return [pl.BlockSpec(memory_space=pltpu.HBM)] * count


def in_hbm(array):
    return pltpu.with_memory_space_constraint(array, pltpu.HBM)


def params(mebibytes):
    return pltpu.CompilerParams(vmem_limit_bytes=mebibytes * 1024 * 1024)


def chip_at(place, row_at):
    turned = row_at ^ (2 * place[3])
    return turned ^ (turned >> 1)


def split_kernel(
    place, count, pairs, innovations, own, ahead1, ahead2, ahead3, held, sems
):
    copies = [pltpu.make_async_copy(pairs, held, sems.at[4])]
    outs = (own, ahead1, ahead2, ahead3)
    for step, out in enumerate(outs):
        at = chip_at(place, (place[2] + step) & 3) * CHIP
        source = innovations.at[:, pl.ds(pl.multiple_of(at, CHIP), CHIP)]
        copies.append(
            pltpu.make_async_copy(source, out.at[:, pl.ds(0, CHIP)], sems.at[step])
        )
    for copy in copies:
        copy.start()
    copies[0].wait()
    left, right = held[0:1, :], held[1:2, :]
    slot = lax.broadcasted_iota(jnp.int32, left.shape, 1)
    live = jnp.where(slot < count[0], left * 24 + (right - left), -1).astype(f32)
    for copy in copies[1:]:
        copy.wait()
    for out in outs:
        out[:, CHIP:] = jnp.full((4, 128), -1.0, f32)
        out[0:1, CHIP : CHIP + live.shape[1]] = live


def split(place, count, pairs, innovations):
    part = jax.ShapeDtypeStruct((4, WIDE), f32)
    return pl.pallas_call(
        split_kernel,
        out_shape=(part, part, part, part),
        in_specs=smem(2) + hbm(2),
        out_specs=vmem(4),
        scratch_shapes=[
            pltpu.VMEM(pairs.shape, jnp.int32),
            pltpu.SemaphoreType.DMA((5,)),
        ],
        compiler_params=params(4),
        name="split",
    )(place, count, in_hbm(pairs), in_hbm(innovations))


def assemble_kernel(place, own, behind1, behind2, behind3, out):
    for y in range(4):
        step = (place[2] - y) & 3
        value = jnp.where(step == 0, own[...], behind1[...])
        value = jnp.where(step == 2, behind2[...], value)
        value = jnp.where(step == 3, behind3[...], value)
        out[4 * y : 4 * y + 4, :] = value


def assemble(place, own, behind1, behind2, behind3):
    return pl.pallas_call(
        assemble_kernel,
        out_shape=jax.ShapeDtypeStruct((16, WIDE), f32),
        in_specs=smem(1) + vmem(4),
        out_specs=vmem(1)[0],
        compiler_params=params(4),
        name="assemble",
    )(place, own, behind1, behind2, behind3)


def pair_flags(row_at, core, mine, other):
    sub = lax.broadcasted_iota(jnp.int32, (8, 128), 0)
    col = lax.broadcasted_iota(jnp.int32, (8, 128), 1)
    far = col < 24
    near = col - lax.div(col, 8) * 8
    ahead = 8 * (lax.div(col, 8) + 1)
    offset = jnp.where(far, ahead + sub - near, jnp.abs(near - sub))
    left_up = jnp.where(far, near, jnp.minimum(near, sub))
    left_down = jnp.where(far, 7 - sub, 7 - jnp.maximum(near, sub))
    left = jnp.where(core == 0, left_up, left_down)
    valid = (offset >= 0) & (offset <= KMAX) & (col < 32)
    target = jnp.where(valid, (row_at * 8 + left) * 24 + offset, -7).astype(f32)
    hit = jnp.zeros((8, 128), f32)
    for source in (mine, other):
        known = source[0:1, CHIP:]
        for y in (1, 2, 3):
            known = jnp.where(row_at == y, source[4 * y : 4 * y + 1, CHIP:], known)
        for i in range(96):
            code = jnp.broadcast_to(known[0:1, i : i + 1], (8, 128))
            hit = jnp.where(code == target, 1.0, hit)
    return jnp.where(hit > 0.5, 0.0, FAR)


def points_kernel(
    place,
    counts,
    all_coords,
    all_std,
    all_variance,
    base,
    aux,
    first,
    right,
    coords,
    std,
    variance,
    sems,
):
    row_at, core = place[0], place[1]
    chip = pl.ds(pl.multiple_of(row_at * CHIP, CHIP), CHIP)
    copies = [
        pltpu.make_async_copy(source.at[:, chip], to, sems.at[i])
        for i, (source, to) in enumerate(
            ((all_coords, coords), (all_std, std), (all_variance, variance))
        )
    ]
    for copy in copies:
        copy.start()
    base[...] = jnp.zeros((8, CHIP), f32)
    for copy in copies:
        copy.wait()
    lane = lax.broadcasted_iota(jnp.int32, (1, BLOCK), 1)
    for j in range(8):
        source = j + core * (7 - 2 * j)
        here = slice(j * BLOCK, (j + 1) * BLOCK)
        region = pl.ds(pl.multiple_of(source * BLOCK, BLOCK), BLOCK)
        live = (lane < counts[row_at * 8 + source]).astype(f32)
        base[0:3, here] = coords[:, region]
        aux[0:1, here] = std[0:1, region] * live
        aux[1:2, here] = variance[0:1, region]
    sub = lax.broadcasted_iota(jnp.int32, (8, CHIP), 0)
    points = base[...]
    side = jnp.where(sub < 3, points * (-GAMMA), jnp.where(sub == 3, GAMMA, 0.0))
    a1, a2, a3 = three_parts(side)
    first[...] = a1
    right[0:16, :] = jnp.concatenate([a2, a2], 0).astype(bf16)
    right[16:32, :] = jnp.concatenate([a1, a3], 0).astype(bf16)


def points(place, counts, coords, std, variance):
    return pl.pallas_call(
        points_kernel,
        out_shape=(
            jax.ShapeDtypeStruct((8, CHIP), f32),
            jax.ShapeDtypeStruct((8, CHIP), f32),
            jax.ShapeDtypeStruct((8, CHIP), f32),
            jax.ShapeDtypeStruct((32, CHIP), bf16),
        ),
        in_specs=smem(2) + hbm(3),
        out_specs=vmem(4),
        scratch_shapes=[
            pltpu.VMEM((3, CHIP), f32),
            pltpu.VMEM((1, CHIP), f32),
            pltpu.VMEM((1, CHIP), f32),
            pltpu.SemaphoreType.DMA((3,)),
        ],
        compiler_params=params(4),
        name="points",
    )(place, counts, in_hbm(coords), in_hbm(std), in_hbm(variance))


def vectors_kernel(place, mine, other, base, aux, halo, vector, flags):
    core = place[1]
    pairs = pair_flags(place[0], core, mine, other)
    flags[...] = pairs
    halo[32:40, 0:CHIP] = base[...]
    halo[32:40, CHIP:] = pairs
    halo[0:32, CHIP:] = jnp.zeros((32, 128), f32)
    for j in range(8):
        here = slice(j * BLOCK, (j + 1) * BLOCK)
        source = (j + core * (7 - 2 * j)) * BLOCK
        local = pl.ds(pl.multiple_of(source, BLOCK), BLOCK)
        spread = aux[0:1, here]
        got, had = other[:, local], mine[:, local]
        for y in range(4):
            rows = slice(4 * y, 4 * y + 4)
            up = jnp.concatenate([had[rows], got[rows]], 0)
            down = jnp.concatenate([got[rows], had[rows]], 0)
            value = jnp.where(core == 0, up, down)
            vector[8 * y : 8 * y + 8, here] = value
            halo[8 * y : 8 * y + 8, here] = value * spread


def vectors(place, mine, other, base, aux):
    return pl.pallas_call(
        vectors_kernel,
        out_shape=(
            jax.ShapeDtypeStruct((40, WIDE), f32),
            jax.ShapeDtypeStruct((ROWS, CHIP), f32),
            jax.ShapeDtypeStruct((8, 128), f32),
        ),
        in_specs=smem(1) + vmem(4),
        out_specs=vmem(3),
        compiler_params=params(4),
        name="vectors",
    )(place, mine, other, base, aux)


def distance(left, right):
    return jnp.maximum(dot(left, right), 1e-30)


def covariance(x):
    z = jnp.maximum(STRETCH - x * lax.rsqrt(x), 0.0)
    z2 = z * z
    return z2 * z2 * (TOP - z)


def sides(count, offset, place, own, halo, first, mask, left, top):
    column = 24 if offset == 0 else 8 * (offset - 1)
    flags = jnp.where(place[1] == 0, own[...], halo[32:40, CHIP:])
    for a in range(8):
        mask[:, a * BLOCK : (a + 1) * BLOCK] = jnp.broadcast_to(
            flags[:, column + a : column + a + 1], (8, BLOCK)
        )
    width = count * BLOCK
    sub = lax.broadcasted_iota(jnp.int32, (8, width), 0)
    points = halo[32:40, 0:width]
    b1, b2, b3 = three_parts(
        jnp.where(sub < 3, points, jnp.where(sub < 5, 1.0, 0.0))
    )
    left[0:width, :] = jnp.concatenate([b1, b2, b1, b2, b3, b1], 0).T.astype(bf16)
    sub = lax.broadcasted_iota(jnp.int32, (8, CHIP), 0)
    a1 = first[...]
    for b in range(count):
        row = jnp.broadcast_to(mask[b : b + 1, :], (8, CHIP))
        top[16 * b : 16 * b + 16, :] = jnp.concatenate(
            [jnp.where(sub == 4, row, a1), a1], 0
        ).astype(bf16)


def side_scratch(count):
    return [
        pltpu.VMEM((8, CHIP), f32),
        pltpu.VMEM((count * BLOCK, 48), bf16),
        pltpu.VMEM((count * 16, CHIP), bf16),
        pltpu.VMEM((2, BLOCK, BLOCK), f32),
    ]


def make_tiles(jobs, left, top, right, high, low, held, total=None):
    def start(n):
        block, here, _, _, _ = jobs[n]
        rows = pl.ds(pl.multiple_of(block * BLOCK, BLOCK), BLOCK)
        upper = pl.ds(pl.multiple_of(block * 16, 16), 16)
        side = jnp.concatenate([top[upper, here], right[:, here]], 0)
        held[n % 2] = distance(left[rows, :], side)

    start(0)
    for n, (_, here, rows, columns, parts) in enumerate(jobs):
        if n + 1 < len(jobs):
            start(n + 1)
        value = covariance(held[n % 2])
        th = value.astype(bf16)
        high[rows, columns] = th
        tl = (value - th.astype(f32)).astype(bf16)
        low[rows, columns] = tl
        if total is not None:
            pair = dot(jnp.concatenate(parts, 0), th)
            total[:, here] += (pair[0:ROWS] + pair[ROWS:]) + dot(parts[0], tl)


def tiles0_kernel(place, own, halo, first, right, high, low, mask, left, top, held):
    sides(4, 0, place, own, halo, first, mask, left, top)
    jobs = []
    for b in range(4):
        for a in range(8):
            here = slice(a * BLOCK, (a + 1) * BLOCK)
            jobs.append((b, here, slice(b * BLOCK, (b + 1) * BLOCK), here, None))
    make_tiles(jobs, left, top, right, high, low, held)


def tiles0(place, own, halo, first, right):
    kept = pltpu.VMEM((HALF, CHIP), bf16)
    return pl.pallas_call(
        tiles0_kernel,
        out_shape=(kept, kept),
        in_specs=smem(1) + vmem(4),
        out_specs=vmem(2),
        scratch_shapes=side_scratch(4),
        compiler_params=params(5),
        name="tiles0",
    )(place, own, halo, first, right)


def tiles_kernel(
    offset,
    place,
    own,
    halo,
    first,
    right,
    before,
    high,
    low,
    total,
    mask,
    left,
    top,
    held,
):
    sides(8, offset, place, own, halo, first, mask, left, top)
    total[...] = before[...]

    def four_blocks(i, carry):
        jobs = []
        for n in range(4):
            b = 4 * i + n
            rows = pl.ds(pl.multiple_of(b * BLOCK, BLOCK), BLOCK)
            parts = two_parts(halo[0:ROWS, rows])
            for a in range(8):
                here = slice(a * BLOCK, (a + 1) * BLOCK)
                jobs.append((b, here, rows, here, parts))
        make_tiles(jobs, left, top, right, high, low, held, total)
        return carry

    lax.fori_loop(0, 2, four_blocks, 0)


def tiles(offset, place, own, halo, first, right, before):
    kept = pltpu.VMEM((CHIP, CHIP), bf16)
    return pl.pallas_call(
        functools.partial(tiles_kernel, offset),
        out_shape=(kept, kept, jax.ShapeDtypeStruct((ROWS, CHIP), f32)),
        in_specs=smem(1) + vmem(5),
        out_specs=vmem(3),
        scratch_shapes=side_scratch(8),
        compiler_params=params(6),
        name=f"tiles{offset}",
    )(place, own, halo, first, right, before)


def edge_kernel(
    place, own, halo, first, right, before, high, low, total, mask, left, top, held
):
    sides(7, 3, place, own, halo, first, mask, left, top)
    total[...] = before[...]
    jobs = []
    for j in range(7):
        rows = slice(j * BLOCK, (j + 1) * BLOCK)
        parts = two_parts(halo[0:ROWS, rows])
        for a in range(j + 1, 8):
            here = slice(a * BLOCK, (a + 1) * BLOCK)
            at = (a * (a - 1) // 2 + j) * BLOCK
            jobs.append((j, here, slice(at, at + BLOCK), slice(0, BLOCK), parts))
    make_tiles(jobs, left, top, right, high, low, held, total)


def edge_tiles(place, own, halo, first, right, before):
    kept = pltpu.VMEM((28 * BLOCK, BLOCK), bf16)
    return pl.pallas_call(
        edge_kernel,
        out_shape=(kept, kept, jax.ShapeDtypeStruct((ROWS, CHIP), f32)),
        in_specs=smem(1) + vmem(5),
        out_specs=vmem(3),
        scratch_shapes=side_scratch(7),
        compiler_params=params(6),
        name="tiles3",
    )(place, own, halo, first, right, before)


def apply_kernel(depth, vector, high, low, before, total):
    uh, ul = two_parts(vector[0:32, 0:depth])
    both = jnp.concatenate([uh, ul], 0)
    for n in range(0, CHIP, 512):
        here = slice(n, n + 512)
        pair = dot(both, high[:, here])
        extra = dot(uh, low[:, here])
        total[:, here] = before[:, here] + ((pair[0:32] + pair[32:64]) + extra)


def apply(vector, high, low, before):
    depth = high.shape[0]
    return pl.pallas_call(
        functools.partial(apply_kernel, depth),
        out_shape=jax.ShapeDtypeStruct((ROWS, CHIP), f32),
        in_specs=vmem(4),
        out_specs=vmem(1)[0],
        compiler_params=params(8),
        name="apply",
    )(vector, high, low, before)


def edge_apply_kernel(vector, high, low, before, total):
    uh, ul = two_parts(vector[0:32, 0 : 7 * BLOCK])
    both = jnp.concatenate([uh, ul], 0)
    total[:, 0:BLOCK] = before[:, 0:BLOCK]
    for a in range(1, 8):
        rows = slice(a * (a - 1) // 2 * BLOCK, a * (a + 1) // 2 * BLOCK)
        here = slice(a * BLOCK, (a + 1) * BLOCK)
        pair = dot(both[:, 0 : a * BLOCK], high[rows, :])
        extra = dot(uh[:, 0 : a * BLOCK], low[rows, :])
        total[:, here] = before[:, here] + ((pair[0:32] + pair[32:64]) + extra)


def edge_apply(vector, high, low, before):
    return pl.pallas_call(
        edge_apply_kernel,
        out_shape=jax.ShapeDtypeStruct((ROWS, CHIP), f32),
        in_specs=vmem(4),
        out_specs=vmem(1)[0],
        compiler_params=params(8),
        name="apply3",
    )(vector, high, low, before)


def combine_kernel(mine, other, aux, vector, image, scaled):
    for j in range(8):
        here = slice(j * BLOCK, (j + 1) * BLOCK)
        there = slice((7 - j) * BLOCK, (8 - j) * BLOCK)
        spread = aux[0:1, here]
        value = (mine[:, here] + other[:, there]) * spread
        value = value + aux[1:2, here] * vector[:, here]
        image[:, here] = value
        scaled[:, here] = value * spread


def combine(mine, other, aux, vector):
    shape = jax.ShapeDtypeStruct((ROWS, CHIP), f32)
    return pl.pallas_call(
        combine_kernel,
        out_shape=(shape, shape),
        in_specs=vmem(4),
        out_specs=vmem(2),
        compiler_params=params(8),
        name="combine",
    )(mine, other, aux, vector)


def finish_kernel(
    place, mine, other, aux, vector, image, own, ahead1, ahead2, ahead3, last, packed
):
    row_at, core = place[2], place[1]
    sums = [jnp.zeros((ROWS, 1), f32) for _ in range(4)]
    for j in range(8):
        here = slice(j * BLOCK, (j + 1) * BLOCK)
        there = slice((7 - j) * BLOCK, (8 - j) * BLOCK)
        start, first = vector[:, here], image[:, here]
        value = (mine[:, here] + other[:, there]) * aux[0:1, here]
        value = value + aux[1:2, here] * first
        last[:, here] = value
        terms = (start * start, start * first, first * first, first * value)
        sums = [s + jnp.sum(t, axis=1, keepdims=True) for s, t in zip(sums, terms)]
    lane = lax.broadcasted_iota(jnp.int32, (ROWS, 128), 1)
    row = jnp.zeros((ROWS, 128), f32)
    for i in range(4):
        row = jnp.where(lane == i, sums[i], row)
    packed[...] = row
    for step, out in enumerate((own, ahead1, ahead2, ahead3)):
        rows = pl.ds(pl.multiple_of(lax.rem(row_at + step, 4) * 8, 8), 8)

        def chosen(value):
            return jnp.where(core == 0, value[0:4], value[4:8])

        for j in range(8):
            here = slice(j * BLOCK, (j + 1) * BLOCK)
            to = (j + core * (7 - 2 * j)) * BLOCK
            out[:, pl.ds(pl.multiple_of(to, BLOCK), BLOCK)] = chosen(image[rows, here])
            out[:, pl.ds(pl.multiple_of(CHIP + to, BLOCK), BLOCK)] = chosen(
                last[rows, here]
            )
        out[:, 2 * CHIP :] = chosen(packed[rows, :])


def finish(place, mine, other, aux, vector, image):
    part = jax.ShapeDtypeStruct((4, 2 * CHIP + 128), f32)
    return pl.pallas_call(
        finish_kernel,
        out_shape=(part, part, part, part),
        in_specs=smem(1) + vmem(5),
        out_specs=vmem(4),
        scratch_shapes=[pltpu.VMEM((ROWS, CHIP), f32), pltpu.VMEM((ROWS, 128), f32)],
        compiler_params=params(6),
        name="finish",
    )(place, mine, other, aux, vector, image)


def region_sums_kernel(own, behind1, behind2, behind3, out):
    total = own[:, 2 * CHIP :] + behind1[:, 2 * CHIP :]
    total = total + (behind2[:, 2 * CHIP :] + behind3[:, 2 * CHIP :])
    out[...] = jnp.broadcast_to(total[None], out.shape)


def region_sums(regions, parts):
    return pl.pallas_call(
        region_sums_kernel,
        out_shape=jax.ShapeDtypeStruct((regions, 4, 128), f32),
        in_specs=vmem(4),
        out_specs=vmem(1)[0],
        compiler_params=params(6),
        name="region_sums",
    )(*parts)


def result_kernel(
    place, sums, innovations, own, behind1, behind2, behind3, field, residual
):
    totals = jnp.sum(sums[...], axis=0)
    bb, bk, kk, kl = (totals[:, i : i + 1] for i in range(4))
    alpha = bb / bk
    norm = alpha * alpha * kk - 2.0 * alpha * bk + bb
    grown = 1.0 + norm / bb
    energy = grown * grown * bk - 2.0 * alpha * grown * kk + alpha * alpha * kl
    step = norm / energy
    for back, part in enumerate((own, behind1, behind2, behind3)):
        at = chip_at(place, (place[2] - back) & 3) * CHIP
        here = pl.ds(pl.multiple_of(at, CHIP), CHIP)
        start = innovations[:, here]
        first, last = part[:, 0:CHIP], part[:, CHIP : 2 * CHIP]
        field[:, here] = alpha * start + step * (grown * start - alpha * first)
        residual[:, here] = (
            start - alpha * first - step * (grown * first - alpha * last)
        )


def result(place, sums, innovations, parts):
    shape = jax.ShapeDtypeStruct(innovations.shape, f32)
    return pl.pallas_call(
        result_kernel,
        out_shape=(shape, shape),
        in_specs=smem(1) + vmem(6),
        out_specs=vmem(2),
        compiler_params=params(6),
        name="result",
    )(place, sums, innovations, *parts)


def device(chip, core):
    region, place = divmod(chip, 4)
    return 8 * region + 2 * (place ^ (place >> 1) ^ (2 * (region % 2))) + core


def neighbours(block, step, chips):
    route = []
    for m in range(chips - step):
        route.append((device(m + step, 0), device(m, 0)))
        route.append((device(m, 1), device(m + step, 1)))
    return lax.ppermute(block, AXES, route)


def sibling(block, chips):
    route = [(i, i ^ 1) for i in range(2 * chips)]
    return lax.ppermute(block, AXES, route)


after = lax.optimization_barrier


def along_y(parts):
    columns = lax.axis_size("cols")
    return [
        lax.ppermute(
            part, "cols", [(i, (i + 2 * step) % columns) for i in range(columns)]
        )
        for step, part in enumerate(parts, 1)
    ]


def per_device(
    innovations, coords, background_std, obs_variance, block_count, pair_list, pair_count
):
    regions = lax.axis_size("region")
    chips = regions * lax.axis_size("cols") // 2
    column = lax.axis_index("cols")
    row_at = column // 2
    odd = lax.axis_index("region") % 2
    turned = row_at ^ (2 * odd)
    place = jnp.stack([turned ^ (turned >> 1), column % 2, row_at, odd])

    own, *ahead = split(place, pair_count, pair_list, innovations)
    behind = along_y(ahead)
    base, aux, first, right = points(
        place,
        block_count,
        coords,
        background_std.reshape(1, -1),
        obs_variance.reshape(1, -1),
    )
    half = assemble(place, own, *behind)
    halo, vector, flags = vectors(place, half, sibling(half, chips), base, aux)

    halos = [neighbours(halo, step, chips) for step in (1, 2, 3)]
    kept = [tiles0(place, flags, halo, first, right)]
    total = apply(halo, *kept[0], jnp.zeros((ROWS, CHIP), f32))
    for k in (1, 2):
        *made, total = tiles(k, place, flags, halos[k - 1], first, right, total)
        kept.append(made)
    *made, part = edge_tiles(place, flags, halos[2], first, right, total)
    kept.append(made)
    image, scaled = combine(part, sibling(part, chips), aux, vector)

    halos = [scaled] + [neighbours(scaled, step, chips) for step in (1, 2, 3)]
    total = jnp.zeros((ROWS, CHIP), f32)
    for k in range(3):
        total = apply(halos[k], *kept[k], total)
    part = edge_apply(halos[3], *kept[3], total)
    own, *ahead = finish(place, part, sibling(part, chips), aux, vector, image)

    parts = [own] + along_y(ahead)
    sums = lax.all_to_all(region_sums(regions, parts), "region", 0, 0, tiled=True)
    return result(place, sums, innovations, parts)


def solution(mesh):
    placed = (
        P("cols", "region"),
        P(None, "region"),
        P("region"),
        P("region"),
        P("region"),
        P(None, ("region", "cols")),
        P(("region", "cols")),
    )
    return jax.shard_map(
        per_device,
        mesh=mesh,
        in_specs=placed,
        out_specs=(P("cols", "region"), P("cols", "region")),
        check_vma=False,
    )
```

```python
import functools

import jax
import jax.numpy as jnp
from jax import lax
from jax.experimental import pallas as pl
from jax.experimental.pallas import tpu as pltpu
from jax.sharding import PartitionSpec as P

BLOCK = 256
KMAX = 23
SUPPORT = 1000.0 / 6371.0

STRETCH = 4.0**0.2
TOP = 5.0 / STRETCH**4
GAMMA = 2.0 * STRETCH**2 / SUPPORT**2
FAR = 2.0**100

ROWS = 32
CHIP = 8 * BLOCK
HALF = 4 * BLOCK
WIDE = CHIP + 128
AXES = ("region", "cols")

bf16 = jnp.bfloat16
f32 = jnp.float32


def dot(a, b):
    return jnp.dot(a, b, preferred_element_type=f32)


def two_parts(x):
    high = x.astype(bf16)
    return high, (x - high.astype(f32)).astype(bf16)


def three_parts(x):
    first = x.astype(bf16).astype(f32)
    rest = x - first
    second = rest.astype(bf16).astype(f32)
    return first, second, (rest - second).astype(bf16).astype(f32)


def vmem(count):
    return [pl.BlockSpec(memory_space=pltpu.VMEM)] * count


def smem(count):
    return [pl.BlockSpec(memory_space=pltpu.SMEM)] * count


def hbm(count):
    return [pl.BlockSpec(memory_space=pltpu.HBM)] * count


def in_hbm(array):
    return pltpu.with_memory_space_constraint(array, pltpu.HBM)


def params(mebibytes):
    return pltpu.CompilerParams(vmem_limit_bytes=mebibytes * 1024 * 1024)


def chip_at(place, row_at):
    turned = row_at ^ (2 * place[3])
    return turned ^ (turned >> 1)


def split_kernel(
    place, count, pairs, innovations, own, ahead1, ahead2, ahead3, held, sems
):
    copies = [pltpu.make_async_copy(pairs, held, sems.at[4])]
    outs = (own, ahead1, ahead2, ahead3)
    for step, out in enumerate(outs):
        at = chip_at(place, (place[2] + step) & 3) * CHIP
        source = innovations.at[:, pl.ds(pl.multiple_of(at, CHIP), CHIP)]
        copies.append(
            pltpu.make_async_copy(source, out.at[:, pl.ds(0, CHIP)], sems.at[step])
        )
    for copy in copies:
        copy.start()
    copies[0].wait()
    left, right = held[0:1, :], held[1:2, :]
    slot = lax.broadcasted_iota(jnp.int32, left.shape, 1)
    live = jnp.where(slot < count[0], left * 24 + (right - left), -1).astype(f32)
    for copy in copies[1:]:
        copy.wait()
    for out in outs:
        out[:, CHIP:] = jnp.full((4, 128), -1.0, f32)
        out[0:1, CHIP : CHIP + live.shape[1]] = live


def split(place, count, pairs, innovations):
    part = jax.ShapeDtypeStruct((4, WIDE), f32)
    return pl.pallas_call(
        split_kernel,
        out_shape=(part, part, part, part),
        in_specs=smem(2) + hbm(2),
        out_specs=vmem(4),
        scratch_shapes=[
            pltpu.VMEM(pairs.shape, jnp.int32),
            pltpu.SemaphoreType.DMA((5,)),
        ],
        compiler_params=params(4),
        name="split",
    )(place, count, in_hbm(pairs), in_hbm(innovations))


def assemble_kernel(place, own, behind1, behind2, behind3, out):
    for y in range(4):
        step = (place[2] - y) & 3
        value = jnp.where(step == 0, own[...], behind1[...])
        value = jnp.where(step == 2, behind2[...], value)
        value = jnp.where(step == 3, behind3[...], value)
        out[4 * y : 4 * y + 4, :] = value


def assemble(place, own, behind1, behind2, behind3):
    return pl.pallas_call(
        assemble_kernel,
        out_shape=jax.ShapeDtypeStruct((16, WIDE), f32),
        in_specs=smem(1) + vmem(4),
        out_specs=vmem(1)[0],
        compiler_params=params(4),
        name="assemble",
    )(place, own, behind1, behind2, behind3)


def pair_flags(row_at, core, mine, other):
    sub = lax.broadcasted_iota(jnp.int32, (8, 128), 0)
    col = lax.broadcasted_iota(jnp.int32, (8, 128), 1)
    far = col < 24
    near = col - lax.div(col, 8) * 8
    ahead = 8 * (lax.div(col, 8) + 1)
    offset = jnp.where(far, ahead + sub - near, jnp.abs(near - sub))
    left_up = jnp.where(far, near, jnp.minimum(near, sub))
    left_down = jnp.where(far, 7 - sub, 7 - jnp.maximum(near, sub))
    left = jnp.where(core == 0, left_up, left_down)
    valid = (offset >= 0) & (offset <= KMAX) & (col < 32)
    target = jnp.where(valid, (row_at * 8 + left) * 24 + offset, -7).astype(f32)
    hit = jnp.zeros((8, 128), f32)
    for source in (mine, other):
        known = source[0:1, CHIP:]
        for y in (1, 2, 3):
            known = jnp.where(row_at == y, source[4 * y : 4 * y + 1, CHIP:], known)
        for i in range(96):
            code = jnp.broadcast_to(known[0:1, i : i + 1], (8, 128))
            hit = jnp.where(code == target, 1.0, hit)
    return jnp.where(hit > 0.5, 0.0, FAR)


def points_kernel(
    place,
    all_counts,
    all_coords,
    all_std,
    all_variance,
    base,
    aux,
    first,
    right,
    coords,
    std,
    variance,
    counts,
    sems,
):
    row_at, core = place[0], place[1]
    chip = pl.ds(pl.multiple_of(row_at * CHIP, CHIP), CHIP)
    copies = [
        pltpu.make_async_copy(source.at[:, chip], to, sems.at[i])
        for i, (source, to) in enumerate(
            ((all_coords, coords), (all_std, std), (all_variance, variance))
        )
    ]
    copies.append(pltpu.make_async_copy(all_counts, counts, sems.at[3]))
    for copy in copies:
        copy.start()
    base[...] = jnp.zeros((8, CHIP), f32)
    for copy in copies:
        copy.wait()
    lane = lax.broadcasted_iota(jnp.int32, (1, BLOCK), 1)
    for j in range(8):
        source = j + core * (7 - 2 * j)
        here = slice(j * BLOCK, (j + 1) * BLOCK)
        region = pl.ds(pl.multiple_of(source * BLOCK, BLOCK), BLOCK)
        live = (lane < counts[row_at * 8 + source]).astype(f32)
        base[0:3, here] = coords[:, region]
        aux[0:1, here] = std[0:1, region] * live
        aux[1:2, here] = variance[0:1, region]
    sub = lax.broadcasted_iota(jnp.int32, (8, CHIP), 0)
    points = base[...]
    side = jnp.where(sub < 3, points * (-GAMMA), jnp.where(sub == 3, GAMMA, 0.0))
    a1, a2, a3 = three_parts(side)
    first[...] = a1
    right[0:16, :] = jnp.concatenate([a2, a2], 0).astype(bf16)
    right[16:32, :] = jnp.concatenate([a1, a3], 0).astype(bf16)


def points(place, counts, coords, std, variance):
    return pl.pallas_call(
        points_kernel,
        out_shape=(
            jax.ShapeDtypeStruct((8, CHIP), f32),
            jax.ShapeDtypeStruct((8, CHIP), f32),
            jax.ShapeDtypeStruct((8, CHIP), f32),
            jax.ShapeDtypeStruct((32, CHIP), bf16),
        ),
        in_specs=smem(1) + hbm(4),
        out_specs=vmem(4),
        scratch_shapes=[
            pltpu.VMEM((3, CHIP), f32),
            pltpu.VMEM((1, CHIP), f32),
            pltpu.VMEM((1, CHIP), f32),
            pltpu.SMEM(counts.shape, jnp.int32),
            pltpu.SemaphoreType.DMA((4,)),
        ],
        compiler_params=params(4),
        name="points",
    )(place, in_hbm(counts), in_hbm(coords), in_hbm(std), in_hbm(variance))


def vectors_kernel(place, mine, other, base, aux, halo, vector, flags):
    core = place[1]
    pairs = pair_flags(place[0], core, mine, other)
    flags[...] = pairs
    halo[32:40, 0:CHIP] = base[...]
    halo[32:40, CHIP:] = pairs
    halo[0:32, CHIP:] = jnp.zeros((32, 128), f32)
    for j in range(8):
        here = slice(j * BLOCK, (j + 1) * BLOCK)
        source = (j + core * (7 - 2 * j)) * BLOCK
        local = pl.ds(pl.multiple_of(source, BLOCK), BLOCK)
        spread = aux[0:1, here]
        got, had = other[:, local], mine[:, local]
        for y in range(4):
            rows = slice(4 * y, 4 * y + 4)
            up = jnp.concatenate([had[rows], got[rows]], 0)
            down = jnp.concatenate([got[rows], had[rows]], 0)
            value = jnp.where(core == 0, up, down)
            vector[8 * y : 8 * y + 8, here] = value
            halo[8 * y : 8 * y + 8, here] = value * spread


def vectors(place, mine, other, base, aux):
    return pl.pallas_call(
        vectors_kernel,
        out_shape=(
            jax.ShapeDtypeStruct((40, WIDE), f32),
            jax.ShapeDtypeStruct((ROWS, CHIP), f32),
            jax.ShapeDtypeStruct((8, 128), f32),
        ),
        in_specs=smem(1) + vmem(4),
        out_specs=vmem(3),
        compiler_params=params(4),
        name="vectors",
    )(place, mine, other, base, aux)


def distance(left, right):
    return jnp.maximum(dot(left, right), 1e-30)


def covariance(x):
    z = jnp.maximum(STRETCH - pl.reciprocal(lax.rsqrt(x), approx=True), 0.0)
    z2 = z * z
    return z2 * z2 * (TOP - z)


def times(parts, tile):
    th, tl = two_parts(tile)
    pair = dot(jnp.concatenate(parts, 0), th)
    return (pair[0:ROWS] + pair[ROWS:]) + dot(parts[0], tl)


def sides(count, offset, place, own, halo, first, mask, left, top):
    column = 24 if offset == 0 else 8 * (offset - 1)
    flags = jnp.where(place[1] == 0, own[...], halo[32:40, CHIP:])
    for a in range(8):
        mask[:, a * BLOCK : (a + 1) * BLOCK] = jnp.broadcast_to(
            flags[:, column + a : column + a + 1], (8, BLOCK)
        )
    width = count * BLOCK
    sub = lax.broadcasted_iota(jnp.int32, (8, width), 0)
    points = halo[32:40, 0:width]
    b1, b2, b3 = three_parts(
        jnp.where(sub < 3, points, jnp.where(sub < 5, 1.0, 0.0))
    )
    left[0:width, :] = jnp.concatenate([b1, b2, b1, b2, b3, b1], 0).T.astype(bf16)
    sub = lax.broadcasted_iota(jnp.int32, (8, CHIP), 0)
    a1 = first[...]
    for b in range(count):
        row = jnp.broadcast_to(mask[b : b + 1, :], (8, CHIP))
        top[16 * b : 16 * b + 16, :] = jnp.concatenate(
            [jnp.where(sub == 4, row, a1), a1], 0
        ).astype(bf16)


def side_scratch(count):
    return [
        pltpu.VMEM((8, CHIP), f32),
        pltpu.VMEM((count * BLOCK, 48), bf16),
        pltpu.VMEM((count * 16, CHIP), bf16),
        pltpu.VMEM((2, BLOCK, BLOCK), f32),
    ]


def make_tiles(jobs, left, top, right, kept, held, total):
    def start(n):
        block, here, _, _, _ = jobs[n]
        rows = pl.ds(pl.multiple_of(block * BLOCK, BLOCK), BLOCK)
        upper = pl.ds(pl.multiple_of(block * 16, 16), 16)
        side = jnp.concatenate([top[upper, here], right[:, here]], 0)
        held[n % 2] = distance(left[rows, :], side)

    start(0)
    for n, (_, here, rows, columns, parts) in enumerate(jobs):
        if n + 1 < len(jobs):
            start(n + 1)
        kept[rows, columns] = covariance(held[n % 2])
        total[:, here] += times(parts, kept[rows, columns])


def tiles0_kernel(
    place, own, halo, first, right, kept, total, mask, left, top, held
):
    sides(4, 0, place, own, halo, first, mask, left, top)
    total[...] = jnp.zeros_like(total)
    jobs = []
    for b in range(4):
        rows = slice(b * BLOCK, (b + 1) * BLOCK)
        parts = two_parts(halo[0:ROWS, rows])
        for a in range(8):
            here = slice(a * BLOCK, (a + 1) * BLOCK)
            jobs.append((b, here, rows, here, parts))
    make_tiles(jobs, left, top, right, kept, held, total)


def tiles0(place, own, halo, first, right):
    return pl.pallas_call(
        tiles0_kernel,
        out_shape=(
            pltpu.VMEM((HALF, CHIP), f32),
            jax.ShapeDtypeStruct((ROWS, CHIP), f32),
        ),
        in_specs=smem(1) + vmem(4),
        out_specs=vmem(2),
        scratch_shapes=side_scratch(4),
        compiler_params=params(3),
        name="tiles0",
    )(place, own, halo, first, right)


def tiles_kernel(
    offset,
    place,
    own,
    halo,
    first,
    right,
    before,
    kept_first,
    kept_last,
    total,
    mask,
    left,
    top,
    held,
):
    sides(8, offset, place, own, halo, first, mask, left, top)
    total[...] = before[...]

    for i, kept in enumerate((kept_first, kept_last)):
        jobs = []
        for n in range(4):
            b = 4 * i + n
            rows = slice(n * BLOCK, (n + 1) * BLOCK)
            parts = two_parts(halo[0:ROWS, b * BLOCK : (b + 1) * BLOCK])
            for a in range(8):
                here = slice(a * BLOCK, (a + 1) * BLOCK)
                jobs.append((b, here, rows, here, parts))
        make_tiles(jobs, left, top, right, kept, held, total)


def tiles(offset, place, own, halo, first, right, before):
    return pl.pallas_call(
        functools.partial(tiles_kernel, offset),
        out_shape=(
            pltpu.VMEM((HALF, CHIP), f32),
            pltpu.VMEM((HALF, CHIP), f32),
            jax.ShapeDtypeStruct((ROWS, CHIP), f32),
        ),
        in_specs=smem(1) + vmem(5),
        out_specs=vmem(3),
        scratch_shapes=side_scratch(8),
        compiler_params=params(4),
        name=f"tiles{offset}",
    )(place, own, halo, first, right, before)


def edge_kernel(
    place, own, halo, first, right, before, kept, total, mask, left, top, held
):
    sides(7, 3, place, own, halo, first, mask, left, top)
    total[...] = before[...]
    jobs = []
    for j in range(7):
        rows = slice(j * BLOCK, (j + 1) * BLOCK)
        parts = two_parts(halo[0:ROWS, rows])
        for a in range(j + 1, 8):
            here = slice(a * BLOCK, (a + 1) * BLOCK)
            at = (a * (a - 1) // 2 + j) * BLOCK
            jobs.append((j, here, slice(at, at + BLOCK), slice(0, BLOCK), parts))
    make_tiles(jobs, left, top, right, kept, held, total)


def edge_tiles(place, own, halo, first, right, before):
    return pl.pallas_call(
        edge_kernel,
        out_shape=(
            pltpu.VMEM((28 * BLOCK, BLOCK), f32),
            jax.ShapeDtypeStruct((ROWS, CHIP), f32),
        ),
        in_specs=smem(1) + vmem(5),
        out_specs=vmem(2),
        scratch_shapes=side_scratch(7),
        compiler_params=params(4),
        name="tiles3",
    )(place, own, halo, first, right, before)


def apply_kernel(vector, *refs):
    *kept, before, total = refs
    uh, ul = two_parts(vector[0:ROWS, 0 : len(kept) * HALF])
    for n in range(0, CHIP, BLOCK):
        here = slice(n, n + BLOCK)
        value = before[:, here]
        for k in range(0, len(kept) * HALF, BLOCK):
            rows = slice(k, k + BLOCK)
            at = k % HALF
            tile = kept[k // HALF][at : at + BLOCK, here]
            value = value + times((uh[:, rows], ul[:, rows]), tile)
        total[:, here] = value


def apply(vector, kept, before):
    return pl.pallas_call(
        apply_kernel,
        out_shape=jax.ShapeDtypeStruct((ROWS, CHIP), f32),
        in_specs=vmem(len(kept) + 2),
        out_specs=vmem(1)[0],
        compiler_params=params(3),
        name="apply",
    )(vector, *kept, before)


def edge_apply_kernel(vector, kept, before, total):
    uh, ul = two_parts(vector[0:ROWS, 0 : 7 * BLOCK])
    total[:, 0:BLOCK] = before[:, 0:BLOCK]
    for a in range(1, 8):
        here = slice(a * BLOCK, (a + 1) * BLOCK)
        value = before[:, here]
        for j in range(a):
            rows = slice(j * BLOCK, (j + 1) * BLOCK)
            at = (a * (a - 1) // 2 + j) * BLOCK
            parts = (uh[:, rows], ul[:, rows])
            value = value + times(parts, kept[at : at + BLOCK, :])
        total[:, here] = value


def edge_apply(vector, kept, before):
    return pl.pallas_call(
        edge_apply_kernel,
        out_shape=jax.ShapeDtypeStruct((ROWS, CHIP), f32),
        in_specs=vmem(3),
        out_specs=vmem(1)[0],
        compiler_params=params(3),
        name="apply3",
    )(vector, kept, before)


def combine_kernel(mine, other, aux, vector, image, scaled):
    for j in range(8):
        here = slice(j * BLOCK, (j + 1) * BLOCK)
        there = slice((7 - j) * BLOCK, (8 - j) * BLOCK)
        spread = aux[0:1, here]
        value = (mine[:, here] + other[:, there]) * spread
        value = value + aux[1:2, here] * vector[:, here]
        image[:, here] = value
        scaled[:, here] = value * spread


def combine(mine, other, aux, vector):
    shape = jax.ShapeDtypeStruct((ROWS, CHIP), f32)
    return pl.pallas_call(
        combine_kernel,
        out_shape=(shape, shape),
        in_specs=vmem(4),
        out_specs=vmem(2),
        compiler_params=params(3),
        name="combine",
    )(mine, other, aux, vector)


def finish_kernel(
    place, mine, other, aux, vector, image, own, ahead1, ahead2, ahead3, last, packed
):
    row_at, core = place[2], place[1]
    sums = [jnp.zeros((ROWS, 1), f32) for _ in range(4)]
    for j in range(8):
        here = slice(j * BLOCK, (j + 1) * BLOCK)
        there = slice((7 - j) * BLOCK, (8 - j) * BLOCK)
        start, first = vector[:, here], image[:, here]
        value = (mine[:, here] + other[:, there]) * aux[0:1, here]
        value = value + aux[1:2, here] * first
        last[:, here] = value
        terms = (start * start, start * first, first * first, first * value)
        sums = [s + jnp.sum(t, axis=1, keepdims=True) for s, t in zip(sums, terms)]
    lane = lax.broadcasted_iota(jnp.int32, (ROWS, 128), 1)
    row = jnp.zeros((ROWS, 128), f32)
    for i in range(4):
        row = jnp.where(lane == i, sums[i], row)
    packed[...] = row
    for step, out in enumerate((own, ahead1, ahead2, ahead3)):
        rows = pl.ds(pl.multiple_of(lax.rem(row_at + step, 4) * 8, 8), 8)

        def chosen(value):
            return jnp.where(core == 0, value[0:4], value[4:8])

        for j in range(8):
            here = slice(j * BLOCK, (j + 1) * BLOCK)
            to = (j + core * (7 - 2 * j)) * BLOCK
            out[:, pl.ds(pl.multiple_of(to, BLOCK), BLOCK)] = chosen(image[rows, here])
            out[:, pl.ds(pl.multiple_of(CHIP + to, BLOCK), BLOCK)] = chosen(
                last[rows, here]
            )
        out[:, 2 * CHIP :] = chosen(packed[rows, :])


def finish(place, mine, other, aux, vector, image):
    part = jax.ShapeDtypeStruct((4, 2 * CHIP + 128), f32)
    return pl.pallas_call(
        finish_kernel,
        out_shape=(part, part, part, part),
        in_specs=smem(1) + vmem(5),
        out_specs=vmem(4),
        scratch_shapes=[pltpu.VMEM((ROWS, CHIP), f32), pltpu.VMEM((ROWS, 128), f32)],
        compiler_params=params(4),
        name="finish",
    )(place, mine, other, aux, vector, image)


def region_sums_kernel(own, behind1, behind2, behind3, out):
    total = own[:, 2 * CHIP :] + behind1[:, 2 * CHIP :]
    total = total + (behind2[:, 2 * CHIP :] + behind3[:, 2 * CHIP :])
    out[...] = jnp.broadcast_to(total[None], out.shape)


def region_sums(regions, parts):
    return pl.pallas_call(
        region_sums_kernel,
        out_shape=jax.ShapeDtypeStruct((regions, 4, 128), f32),
        in_specs=vmem(4),
        out_specs=vmem(1)[0],
        compiler_params=params(4),
        name="region_sums",
    )(*parts)


def result_kernel(
    place, sums, innovations, own, behind1, behind2, behind3, field, residual
):
    totals = jnp.sum(sums[...], axis=0)
    bb, bk, kk, kl = (totals[:, i : i + 1] for i in range(4))
    alpha = bb / bk
    norm = alpha * alpha * kk - 2.0 * alpha * bk + bb
    grown = 1.0 + norm / bb
    energy = grown * grown * bk - 2.0 * alpha * grown * kk + alpha * alpha * kl
    step = norm / energy
    for back, part in enumerate((own, behind1, behind2, behind3)):
        at = chip_at(place, (place[2] - back) & 3) * CHIP
        here = pl.ds(pl.multiple_of(at, CHIP), CHIP)
        start = innovations[:, here]
        first, last = part[:, 0:CHIP], part[:, CHIP : 2 * CHIP]
        field[:, here] = alpha * start + step * (grown * start - alpha * first)
        residual[:, here] = (
            start - alpha * first - step * (grown * first - alpha * last)
        )


def result(place, sums, innovations, parts):
    shape = jax.ShapeDtypeStruct(innovations.shape, f32)
    return pl.pallas_call(
        result_kernel,
        out_shape=(shape, shape),
        in_specs=smem(1) + vmem(6),
        out_specs=vmem(2),
        compiler_params=params(4),
        name="result",
    )(place, sums, innovations, *parts)


def device(chip, core):
    region, place = divmod(chip, 4)
    return 8 * region + 2 * (place ^ (place >> 1) ^ (2 * (region % 2))) + core


def neighbours(block, step, chips):
    route = []
    for m in range(chips - step):
        route.append((device(m + step, 0), device(m, 0)))
        route.append((device(m, 1), device(m + step, 1)))
    return lax.ppermute(block, AXES, route)


def sibling(block, chips):
    route = [(i, i ^ 1) for i in range(2 * chips)]
    return lax.ppermute(block, AXES, route)


after = lax.optimization_barrier


def along_y(parts):
    columns = lax.axis_size("cols")
    return [
        lax.ppermute(
            part, "cols", [(i, (i + 2 * step) % columns) for i in range(columns)]
        )
        for step, part in enumerate(parts, 1)
    ]


def per_device(
    innovations, coords, background_std, obs_variance, block_count, pair_list, pair_count
):
    regions = lax.axis_size("region")
    chips = regions * lax.axis_size("cols") // 2
    column = lax.axis_index("cols")
    row_at = column // 2
    odd = lax.axis_index("region") % 2
    turned = row_at ^ (2 * odd)
    place = jnp.stack([turned ^ (turned >> 1), column % 2, row_at, odd])

    own, *ahead = split(place, pair_count, pair_list, innovations)
    behind = along_y(ahead)
    base, aux, first, right = points(
        place,
        block_count,
        coords,
        background_std.reshape(1, -1),
        obs_variance.reshape(1, -1),
    )
    behind, base, aux = after((behind, base, aux))
    half = assemble(place, own, *behind)
    halo, vector, flags = vectors(place, half, sibling(half, chips), base, aux)

    halos = [neighbours(halo, step, chips) for step in (1, 2, 3)]
    *made, total = tiles0(place, flags, halo, first, right)
    kept = [made]
    for k in (1, 2):
        *made, total = tiles(k, place, flags, halos[k - 1], first, right, total)
        kept.append(made)
    made, part = edge_tiles(place, flags, halos[2], first, right, total)
    kept.append(made)
    image, scaled = combine(part, sibling(part, chips), aux, vector)

    halos = [scaled] + [neighbours(scaled, step, chips) for step in (1, 2, 3)]
    total = jnp.zeros((ROWS, CHIP), f32)
    for k in range(3):
        total = apply(halos[k], kept[k], total)
    part = edge_apply(halos[3], kept[3], total)
    own, *ahead = finish(place, part, sibling(part, chips), aux, vector, image)

    parts = [own] + along_y(ahead)
    sums = lax.all_to_all(region_sums(regions, parts), "region", 0, 0, tiled=True)
    return result(place, sums, innovations, parts)


def solution(mesh):
    placed = (
        P("cols", "region"),
        P(None, "region"),
        P("region"),
        P("region"),
        P("region"),
        P(None, ("region", "cols")),
        P(("region", "cols")),
    )
    return jax.shard_map(
        per_device,
        mesh=mesh,
        in_specs=placed,
        out_specs=(P("cols", "region"), P("cols", "region")),
        check_vma=False,
    )
```

```python
import functools

import jax
import jax.numpy as jnp
from jax import lax
from jax.experimental import pallas as pl
from jax.experimental.pallas import tpu as pltpu
from jax.sharding import PartitionSpec as P

BLOCK = 256
KMAX = 23
SUPPORT = 1000.0 / 6371.0

STRETCH = 4.0**0.2
TOP = 5.0 / STRETCH**4
GAMMA = 2.0 * STRETCH**2 / SUPPORT**2
FAR = 2.0**100

ROWS = 32
CHIP = 8 * BLOCK
HALF = 4 * BLOCK
WIDE = CHIP + 128
AXES = ("region", "cols")

bf16 = jnp.bfloat16
f32 = jnp.float32


def dot(a, b):
    return jnp.dot(a, b, preferred_element_type=f32)


def two_parts(x):
    high = x.astype(bf16)
    return high, (x - high.astype(f32)).astype(bf16)


def three_parts(x):
    first = x.astype(bf16).astype(f32)
    rest = x - first
    second = rest.astype(bf16).astype(f32)
    return first, second, (rest - second).astype(bf16).astype(f32)


def vmem(count):
    return [pl.BlockSpec(memory_space=pltpu.VMEM)] * count


def smem(count):
    return [pl.BlockSpec(memory_space=pltpu.SMEM)] * count


def hbm(count):
    return [pl.BlockSpec(memory_space=pltpu.HBM)] * count


def in_hbm(array):
    return pltpu.with_memory_space_constraint(array, pltpu.HBM)


def params(mebibytes):
    return pltpu.CompilerParams(vmem_limit_bytes=mebibytes * 1024 * 1024)


def chip_at(place, row_at):
    turned = row_at ^ (2 * place[3])
    return turned ^ (turned >> 1)


def split_kernel(
    place, count, pairs, innovations, own, ahead1, ahead2, ahead3, held, sems
):
    copies = [pltpu.make_async_copy(pairs, held, sems.at[4])]
    outs = (own, ahead1, ahead2, ahead3)
    for step, out in enumerate(outs):
        at = chip_at(place, (place[2] + step) & 3) * CHIP
        source = innovations.at[:, pl.ds(pl.multiple_of(at, CHIP), CHIP)]
        copies.append(
            pltpu.make_async_copy(source, out.at[:, pl.ds(0, CHIP)], sems.at[step])
        )
    for copy in copies:
        copy.start()
    copies[0].wait()
    left, right = held[0:1, :], held[1:2, :]
    slot = lax.broadcasted_iota(jnp.int32, left.shape, 1)
    live = jnp.where(slot < count[0], left * 24 + (right - left), -1).astype(f32)
    for copy in copies[1:]:
        copy.wait()
    for out in outs:
        out[:, CHIP:] = jnp.full((4, 128), -1.0, f32)
        out[0:1, CHIP : CHIP + live.shape[1]] = live


def split(place, count, pairs, innovations):
    part = jax.ShapeDtypeStruct((4, WIDE), f32)
    return pl.pallas_call(
        split_kernel,
        out_shape=(part, part, part, part),
        in_specs=smem(2) + hbm(2),
        out_specs=vmem(4),
        scratch_shapes=[
            pltpu.VMEM(pairs.shape, jnp.int32),
            pltpu.SemaphoreType.DMA((5,)),
        ],
        compiler_params=params(4),
        name="split",
    )(place, count, in_hbm(pairs), in_hbm(innovations))


def assemble_kernel(place, own, behind1, behind2, behind3, out):
    for y in range(4):
        step = (place[2] - y) & 3
        value = jnp.where(step == 0, own[...], behind1[...])
        value = jnp.where(step == 2, behind2[...], value)
        value = jnp.where(step == 3, behind3[...], value)
        out[4 * y : 4 * y + 4, :] = value


def assemble(place, own, behind1, behind2, behind3):
    return pl.pallas_call(
        assemble_kernel,
        out_shape=jax.ShapeDtypeStruct((16, WIDE), f32),
        in_specs=smem(1) + vmem(4),
        out_specs=vmem(1)[0],
        compiler_params=params(4),
        name="assemble",
    )(place, own, behind1, behind2, behind3)


def pair_flags(row_at, core, mine, other):
    sub = lax.broadcasted_iota(jnp.int32, (8, 128), 0)
    col = lax.broadcasted_iota(jnp.int32, (8, 128), 1)
    far = col < 24
    near = col - lax.div(col, 8) * 8
    ahead = 8 * (lax.div(col, 8) + 1)
    offset = jnp.where(far, ahead + sub - near, jnp.abs(near - sub))
    left_up = jnp.where(far, near, jnp.minimum(near, sub))
    left_down = jnp.where(far, 7 - sub, 7 - jnp.maximum(near, sub))
    left = jnp.where(core == 0, left_up, left_down)
    valid = (offset >= 0) & (offset <= KMAX) & (col < 32)
    target = jnp.where(valid, (row_at * 8 + left) * 24 + offset, -7).astype(f32)
    hit = jnp.zeros((8, 128), f32)
    for source in (mine, other):
        known = source[0:1, CHIP:]
        for y in (1, 2, 3):
            known = jnp.where(row_at == y, source[4 * y : 4 * y + 1, CHIP:], known)
        for i in range(96):
            code = jnp.broadcast_to(known[0:1, i : i + 1], (8, 128))
            hit = jnp.where(code == target, 1.0, hit)
    return jnp.where(hit > 0.5, 0.0, FAR)


def points_kernel(
    place,
    all_counts,
    all_coords,
    all_std,
    all_variance,
    base,
    aux,
    first,
    right,
    coords,
    std,
    variance,
    counts,
    sems,
):
    row_at, core = place[0], place[1]
    chip = pl.ds(pl.multiple_of(row_at * CHIP, CHIP), CHIP)
    copies = [
        pltpu.make_async_copy(source.at[:, chip], to, sems.at[i])
        for i, (source, to) in enumerate(
            ((all_coords, coords), (all_std, std), (all_variance, variance))
        )
    ]
    copies.append(pltpu.make_async_copy(all_counts, counts, sems.at[3]))
    for copy in copies:
        copy.start()
    base[...] = jnp.zeros((8, CHIP), f32)
    for copy in copies:
        copy.wait()
    lane = lax.broadcasted_iota(jnp.int32, (1, BLOCK), 1)
    for j in range(8):
        source = j + core * (7 - 2 * j)
        here = slice(j * BLOCK, (j + 1) * BLOCK)
        region = pl.ds(pl.multiple_of(source * BLOCK, BLOCK), BLOCK)
        live = (lane < counts[row_at * 8 + source]).astype(f32)
        base[0:3, here] = coords[:, region]
        aux[0:1, here] = std[0:1, region] * live
        aux[1:2, here] = variance[0:1, region]
    sub = lax.broadcasted_iota(jnp.int32, (8, CHIP), 0)
    points = base[...]
    side = jnp.where(sub < 3, points * (-GAMMA), jnp.where(sub == 3, GAMMA, 0.0))
    a1, a2, a3 = three_parts(side)
    first[...] = a1
    right[0:16, :] = jnp.concatenate([a2, a2], 0).astype(bf16)
    right[16:32, :] = jnp.concatenate([a1, a3], 0).astype(bf16)


def points(place, counts, coords, std, variance):
    return pl.pallas_call(
        points_kernel,
        out_shape=(
            jax.ShapeDtypeStruct((8, CHIP), f32),
            jax.ShapeDtypeStruct((8, CHIP), f32),
            jax.ShapeDtypeStruct((8, CHIP), f32),
            jax.ShapeDtypeStruct((32, CHIP), bf16),
        ),
        in_specs=smem(1) + hbm(4),
        out_specs=vmem(4),
        scratch_shapes=[
            pltpu.VMEM((3, CHIP), f32),
            pltpu.VMEM((1, CHIP), f32),
            pltpu.VMEM((1, CHIP), f32),
            pltpu.SMEM(counts.shape, jnp.int32),
            pltpu.SemaphoreType.DMA((4,)),
        ],
        compiler_params=params(4),
        name="points",
    )(place, in_hbm(counts), in_hbm(coords), in_hbm(std), in_hbm(variance))


def vectors_kernel(place, mine, other, base, aux, halo, vector, flags):
    core = place[1]
    pairs = pair_flags(place[0], core, mine, other)
    flags[...] = pairs
    halo[32:40, 0:CHIP] = base[...]
    halo[32:40, CHIP:] = pairs
    halo[0:32, CHIP:] = jnp.zeros((32, 128), f32)
    for j in range(8):
        here = slice(j * BLOCK, (j + 1) * BLOCK)
        source = (j + core * (7 - 2 * j)) * BLOCK
        local = pl.ds(pl.multiple_of(source, BLOCK), BLOCK)
        spread = aux[0:1, here]
        got, had = other[:, local], mine[:, local]
        for y in range(4):
            rows = slice(4 * y, 4 * y + 4)
            up = jnp.concatenate([had[rows], got[rows]], 0)
            down = jnp.concatenate([got[rows], had[rows]], 0)
            value = jnp.where(core == 0, up, down)
            vector[8 * y : 8 * y + 8, here] = value
            halo[8 * y : 8 * y + 8, here] = value * spread


def vectors(place, mine, other, base, aux):
    return pl.pallas_call(
        vectors_kernel,
        out_shape=(
            jax.ShapeDtypeStruct((40, WIDE), f32),
            jax.ShapeDtypeStruct((ROWS, CHIP), f32),
            jax.ShapeDtypeStruct((8, 128), f32),
        ),
        in_specs=smem(1) + vmem(4),
        out_specs=vmem(3),
        compiler_params=params(4),
        name="vectors",
    )(place, mine, other, base, aux)


def distance(left, right):
    return jnp.maximum(dot(left, right), 1e-30)


def covariance(x):
    z = jnp.maximum(STRETCH - pl.reciprocal(lax.rsqrt(x), approx=True), 0.0)
    z2 = z * z
    return z2 * z2 * (TOP - z)


def times(parts, tile):
    th, tl = two_parts(tile)
    pair = dot(jnp.concatenate(parts, 0), th)
    return (pair[0:ROWS] + pair[ROWS:]) + dot(parts[0], tl)


def sides(count, offset, place, own, halo, first, mask, left, top):
    column = 24 if offset == 0 else 8 * (offset - 1)
    flags = jnp.where(place[1] == 0, own[...], halo[32:40, CHIP:])
    for a in range(8):
        mask[:, a * BLOCK : (a + 1) * BLOCK] = jnp.broadcast_to(
            flags[:, column + a : column + a + 1], (8, BLOCK)
        )
    width = count * BLOCK
    sub = lax.broadcasted_iota(jnp.int32, (8, width), 0)
    points = halo[32:40, 0:width]
    b1, b2, b3 = three_parts(
        jnp.where(sub < 3, points, jnp.where(sub < 5, 1.0, 0.0))
    )
    left[0:width, :] = jnp.concatenate([b1, b2, b1, b2, b3, b1], 0).T.astype(bf16)
    sub = lax.broadcasted_iota(jnp.int32, (8, CHIP), 0)
    a1 = first[...]
    for b in range(count):
        row = jnp.broadcast_to(mask[b : b + 1, :], (8, CHIP))
        top[16 * b : 16 * b + 16, :] = jnp.concatenate(
            [jnp.where(sub == 4, row, a1), a1], 0
        ).astype(bf16)


def side_scratch(count):
    return [
        pltpu.VMEM((8, CHIP), f32),
        pltpu.VMEM((count * BLOCK, 48), bf16),
        pltpu.VMEM((count * 16, CHIP), bf16),
        pltpu.VMEM((2, BLOCK, BLOCK), f32),
    ]


def make_tiles(jobs, left, top, right, kept, held, total):
    def start(n):
        block, here, _, _, _ = jobs[n]
        rows = pl.ds(pl.multiple_of(block * BLOCK, BLOCK), BLOCK)
        upper = pl.ds(pl.multiple_of(block * 16, 16), 16)
        side = jnp.concatenate([top[upper, here], right[:, here]], 0)
        held[n % 2] = distance(left[rows, :], side)

    start(0)
    for n, (_, here, rows, columns, parts) in enumerate(jobs):
        if n + 1 < len(jobs):
            start(n + 1)
        kept[rows, columns] = covariance(held[n % 2])
        total[:, here] += times(parts, kept[rows, columns])


def tiles0_kernel(
    place, own, halo, first, right, kept, total, mask, left, top, held
):
    sides(4, 0, place, own, halo, first, mask, left, top)
    total[...] = jnp.zeros_like(total)
    jobs = []
    for b in range(4):
        rows = slice(b * BLOCK, (b + 1) * BLOCK)
        parts = two_parts(halo[0:ROWS, rows])
        for a in range(8):
            here = slice(a * BLOCK, (a + 1) * BLOCK)
            jobs.append((b, here, rows, here, parts))
    make_tiles(jobs, left, top, right, kept, held, total)


def tiles0(place, own, halo, first, right):
    return pl.pallas_call(
        tiles0_kernel,
        out_shape=(
            pltpu.VMEM((HALF, CHIP), f32),
            jax.ShapeDtypeStruct((ROWS, CHIP), f32),
        ),
        in_specs=smem(1) + vmem(4),
        out_specs=vmem(2),
        scratch_shapes=side_scratch(4),
        compiler_params=params(3),
        name="tiles0",
    )(place, own, halo, first, right)


def tiles_kernel(
    offset,
    place,
    own,
    halo,
    first,
    right,
    before,
    kept,
    total,
    mask,
    left,
    top,
    held,
):
    sides(8, offset, place, own, halo, first, mask, left, top)
    total[...] = before[...]

    def four_blocks(i, carry):
        jobs = []
        for n in range(4):
            b = 4 * i + n
            rows = pl.ds(pl.multiple_of(b * BLOCK, BLOCK), BLOCK)
            parts = two_parts(halo[0:ROWS, rows])
            for a in range(8):
                here = slice(a * BLOCK, (a + 1) * BLOCK)
                jobs.append((b, here, rows, here, parts))
        make_tiles(jobs, left, top, right, kept, held, total)
        return carry

    lax.fori_loop(0, 2, four_blocks, 0)


def tiles(offset, place, own, halo, first, right, before):
    return pl.pallas_call(
        functools.partial(tiles_kernel, offset),
        out_shape=(
            pltpu.VMEM((CHIP, CHIP), f32),
            jax.ShapeDtypeStruct((ROWS, CHIP), f32),
        ),
        in_specs=smem(1) + vmem(5),
        out_specs=vmem(2),
        scratch_shapes=side_scratch(8),
        compiler_params=params(4),
        name=f"tiles{offset}",
    )(place, own, halo, first, right, before)


def edge_kernel(
    place, own, halo, first, right, before, kept, total, mask, left, top, held
):
    sides(7, 3, place, own, halo, first, mask, left, top)
    total[...] = before[...]
    jobs = []
    for j in range(7):
        rows = slice(j * BLOCK, (j + 1) * BLOCK)
        parts = two_parts(halo[0:ROWS, rows])
        for a in range(j + 1, 8):
            here = slice(a * BLOCK, (a + 1) * BLOCK)
            at = (a * (a - 1) // 2 + j) * BLOCK
            jobs.append((j, here, slice(at, at + BLOCK), slice(0, BLOCK), parts))
    make_tiles(jobs, left, top, right, kept, held, total)


def edge_tiles(place, own, halo, first, right, before):
    return pl.pallas_call(
        edge_kernel,
        out_shape=(
            pltpu.VMEM((28 * BLOCK, BLOCK), f32),
            jax.ShapeDtypeStruct((ROWS, CHIP), f32),
        ),
        in_specs=smem(1) + vmem(5),
        out_specs=vmem(2),
        scratch_shapes=side_scratch(7),
        compiler_params=params(4),
        name="tiles3",
    )(place, own, halo, first, right, before)


def apply_kernel(depth, vector, kept, before, total):
    uh, ul = two_parts(vector[0:ROWS, 0:depth])

    def half(i, carry):
        for n in range(0, HALF, BLOCK):
            here = pl.ds(pl.multiple_of(i * HALF + n, BLOCK), BLOCK)
            value = before[:, here]
            for k in range(0, depth, BLOCK):
                rows = slice(k, k + BLOCK)
                value = value + times((uh[:, rows], ul[:, rows]), kept[rows, here])
            total[:, here] = value
        return carry

    lax.fori_loop(0, CHIP // HALF, half, 0)


def apply(vector, kept, before):
    return pl.pallas_call(
        functools.partial(apply_kernel, kept.shape[0]),
        out_shape=jax.ShapeDtypeStruct((ROWS, CHIP), f32),
        in_specs=vmem(3),
        out_specs=vmem(1)[0],
        compiler_params=params(3),
        name="apply",
    )(vector, kept, before)


def edge_apply_kernel(vector, kept, before, total):
    uh, ul = two_parts(vector[0:ROWS, 0 : 7 * BLOCK])
    total[:, 0:BLOCK] = before[:, 0:BLOCK]
    for a in range(1, 8):
        here = slice(a * BLOCK, (a + 1) * BLOCK)
        value = before[:, here]
        for j in range(a):
            rows = slice(j * BLOCK, (j + 1) * BLOCK)
            at = (a * (a - 1) // 2 + j) * BLOCK
            parts = (uh[:, rows], ul[:, rows])
            value = value + times(parts, kept[at : at + BLOCK, :])
        total[:, here] = value


def edge_apply(vector, kept, before):
    return pl.pallas_call(
        edge_apply_kernel,
        out_shape=jax.ShapeDtypeStruct((ROWS, CHIP), f32),
        in_specs=vmem(3),
        out_specs=vmem(1)[0],
        compiler_params=params(3),
        name="apply3",
    )(vector, kept, before)


def combine_kernel(mine, other, aux, vector, image, scaled):
    for j in range(8):
        here = slice(j * BLOCK, (j + 1) * BLOCK)
        there = slice((7 - j) * BLOCK, (8 - j) * BLOCK)
        spread = aux[0:1, here]
        value = (mine[:, here] + other[:, there]) * spread
        value = value + aux[1:2, here] * vector[:, here]
        image[:, here] = value
        scaled[:, here] = value * spread


def combine(mine, other, aux, vector):
    shape = jax.ShapeDtypeStruct((ROWS, CHIP), f32)
    return pl.pallas_call(
        combine_kernel,
        out_shape=(shape, shape),
        in_specs=vmem(4),
        out_specs=vmem(2),
        compiler_params=params(3),
        name="combine",
    )(mine, other, aux, vector)


def finish_kernel(
    place, mine, other, aux, vector, image, own, ahead1, ahead2, ahead3, last, packed
):
    row_at, core = place[2], place[1]
    sums = [jnp.zeros((ROWS, 1), f32) for _ in range(4)]
    for j in range(8):
        here = slice(j * BLOCK, (j + 1) * BLOCK)
        there = slice((7 - j) * BLOCK, (8 - j) * BLOCK)
        start, first = vector[:, here], image[:, here]
        value = (mine[:, here] + other[:, there]) * aux[0:1, here]
        value = value + aux[1:2, here] * first
        last[:, here] = value
        terms = (start * start, start * first, first * first, first * value)
        sums = [s + jnp.sum(t, axis=1, keepdims=True) for s, t in zip(sums, terms)]
    lane = lax.broadcasted_iota(jnp.int32, (ROWS, 128), 1)
    row = jnp.zeros((ROWS, 128), f32)
    for i in range(4):
        row = jnp.where(lane == i, sums[i], row)
    packed[...] = row
    for step, out in enumerate((own, ahead1, ahead2, ahead3)):
        rows = pl.ds(pl.multiple_of(lax.rem(row_at + step, 4) * 8, 8), 8)

        def chosen(value):
            return jnp.where(core == 0, value[0:4], value[4:8])

        for j in range(8):
            here = slice(j * BLOCK, (j + 1) * BLOCK)
            to = (j + core * (7 - 2 * j)) * BLOCK
            out[:, pl.ds(pl.multiple_of(to, BLOCK), BLOCK)] = chosen(image[rows, here])
            out[:, pl.ds(pl.multiple_of(CHIP + to, BLOCK), BLOCK)] = chosen(
                last[rows, here]
            )
        out[:, 2 * CHIP :] = chosen(packed[rows, :])


def finish(place, mine, other, aux, vector, image):
    part = jax.ShapeDtypeStruct((4, 2 * CHIP + 128), f32)
    return pl.pallas_call(
        finish_kernel,
        out_shape=(part, part, part, part),
        in_specs=smem(1) + vmem(5),
        out_specs=vmem(4),
        scratch_shapes=[pltpu.VMEM((ROWS, CHIP), f32), pltpu.VMEM((ROWS, 128), f32)],
        compiler_params=params(4),
        name="finish",
    )(place, mine, other, aux, vector, image)


def region_sums_kernel(own, behind1, behind2, behind3, out):
    total = own[:, 2 * CHIP :] + behind1[:, 2 * CHIP :]
    total = total + (behind2[:, 2 * CHIP :] + behind3[:, 2 * CHIP :])
    out[...] = jnp.broadcast_to(total[None], out.shape)


def region_sums(regions, parts):
    return pl.pallas_call(
        region_sums_kernel,
        out_shape=jax.ShapeDtypeStruct((regions, 4, 128), f32),
        in_specs=vmem(4),
        out_specs=vmem(1)[0],
        compiler_params=params(4),
        name="region_sums",
    )(*parts)


def result_kernel(
    place, sums, innovations, own, behind1, behind2, behind3, field, residual
):
    totals = jnp.sum(sums[...], axis=0)
    bb, bk, kk, kl = (totals[:, i : i + 1] for i in range(4))
    alpha = bb / bk
    norm = alpha * alpha * kk - 2.0 * alpha * bk + bb
    grown = 1.0 + norm / bb
    energy = grown * grown * bk - 2.0 * alpha * grown * kk + alpha * alpha * kl
    step = norm / energy
    for back, part in enumerate((own, behind1, behind2, behind3)):
        at = chip_at(place, (place[2] - back) & 3) * CHIP
        here = pl.ds(pl.multiple_of(at, CHIP), CHIP)
        start = innovations[:, here]
        first, last = part[:, 0:CHIP], part[:, CHIP : 2 * CHIP]
        field[:, here] = alpha * start + step * (grown * start - alpha * first)
        residual[:, here] = (
            start - alpha * first - step * (grown * first - alpha * last)
        )


def result(place, sums, innovations, parts):
    shape = jax.ShapeDtypeStruct(innovations.shape, f32)
    return pl.pallas_call(
        result_kernel,
        out_shape=(shape, shape),
        in_specs=smem(1) + vmem(6),
        out_specs=vmem(2),
        compiler_params=params(4),
        name="result",
    )(place, sums, innovations, *parts)


def device(chip, core):
    region, place = divmod(chip, 4)
    return 8 * region + 2 * (place ^ (place >> 1) ^ (2 * (region % 2))) + core


def neighbours(block, step, chips):
    route = []
    for m in range(chips - step):
        route.append((device(m + step, 0), device(m, 0)))
        route.append((device(m, 1), device(m + step, 1)))
    return lax.ppermute(block, AXES, route)


def sibling(block, chips):
    route = [(i, i ^ 1) for i in range(2 * chips)]
    return lax.ppermute(block, AXES, route)


after = lax.optimization_barrier


def along_y(parts):
    columns = lax.axis_size("cols")
    return [
        lax.ppermute(
            part, "cols", [(i, (i + 2 * step) % columns) for i in range(columns)]
        )
        for step, part in enumerate(parts, 1)
    ]


def per_device(
    innovations, coords, background_std, obs_variance, block_count, pair_list, pair_count
):
    regions = lax.axis_size("region")
    chips = regions * lax.axis_size("cols") // 2
    column = lax.axis_index("cols")
    row_at = column // 2
    odd = lax.axis_index("region") % 2
    turned = row_at ^ (2 * odd)
    place = jnp.stack([turned ^ (turned >> 1), column % 2, row_at, odd])

    own, *ahead = split(place, pair_count, pair_list, innovations)
    behind = along_y(ahead)
    base, aux, first, right = points(
        place,
        block_count,
        coords,
        background_std.reshape(1, -1),
        obs_variance.reshape(1, -1),
    )
    behind, base, aux = after((behind, base, aux))
    half = assemble(place, own, *behind)
    halo, vector, flags = vectors(place, half, sibling(half, chips), base, aux)

    halos = [neighbours(halo, step, chips) for step in (1, 2, 3)]
    made, total = tiles0(place, flags, halo, first, right)
    kept = [made]
    for k in (1, 2):
        made, total = tiles(k, place, flags, halos[k - 1], first, right, total)
        kept.append(made)
    made, part = edge_tiles(place, flags, halos[2], first, right, total)
    kept.append(made)
    image, scaled = combine(part, sibling(part, chips), aux, vector)

    halos = [scaled] + [neighbours(scaled, step, chips) for step in (1, 2, 3)]
    total = jnp.zeros((ROWS, CHIP), f32)
    for k in range(3):
        total = apply(halos[k], kept[k], total)
    part = edge_apply(halos[3], kept[3], total)
    own, *ahead = finish(place, part, sibling(part, chips), aux, vector, image)

    parts = [own] + along_y(ahead)
    sums = lax.all_to_all(region_sums(regions, parts), "region", 0, 0, tiled=True)
    return result(place, sums, innovations, parts)


def solution(mesh):
    placed = (
        P("cols", "region"),
        P(None, "region"),
        P("region"),
        P("region"),
        P("region"),
        P(None, ("region", "cols")),
        P(("region", "cols")),
    )
    return jax.shard_map(
        per_device,
        mesh=mesh,
        in_specs=placed,
        out_specs=(P("cols", "region"), P("cols", "region")),
        check_vma=False,
    )
```

```python
import functools

import jax
import jax.numpy as jnp
from jax import lax
from jax.experimental import pallas as pl
from jax.experimental.pallas import tpu as pltpu
from jax.sharding import PartitionSpec as P

BLOCK = 256
KMAX = 23
SUPPORT = 1000.0 / 6371.0

STRETCH = 4.0**0.2
TOP = 5.0 / STRETCH**4
GAMMA = 2.0 * STRETCH**2 / SUPPORT**2
FAR = 2.0**100

ROWS = 32
CHIP = 8 * BLOCK
HALF = 4 * BLOCK
WIDE = CHIP + 128
AXES = ("region", "cols")

bf16 = jnp.bfloat16
f32 = jnp.float32


def dot(a, b):
    return jnp.dot(a, b, preferred_element_type=f32)


def two_parts(x):
    high = x.astype(bf16)
    return high, (x - high.astype(f32)).astype(bf16)


def three_parts(x):
    first = x.astype(bf16).astype(f32)
    rest = x - first
    second = rest.astype(bf16).astype(f32)
    return first, second, (rest - second).astype(bf16).astype(f32)


def vmem(count):
    return [pl.BlockSpec(memory_space=pltpu.VMEM)] * count


def smem(count):
    return [pl.BlockSpec(memory_space=pltpu.SMEM)] * count


def hbm(count):
    return [pl.BlockSpec(memory_space=pltpu.HBM)] * count


def in_hbm(array):
    return pltpu.with_memory_space_constraint(array, pltpu.HBM)


def params(mebibytes):
    return pltpu.CompilerParams(vmem_limit_bytes=mebibytes * 1024 * 1024)


def chip_at(place, row_at):
    turned = row_at ^ (2 * place[3])
    return turned ^ (turned >> 1)


def split_kernel(
    place, count, pairs, innovations, own, ahead1, ahead2, ahead3, held, sems
):
    copies = [pltpu.make_async_copy(pairs, held, sems.at[4])]
    outs = (own, ahead1, ahead2, ahead3)
    for step, out in enumerate(outs):
        at = chip_at(place, (place[2] + step) & 3) * CHIP
        source = innovations.at[:, pl.ds(pl.multiple_of(at, CHIP), CHIP)]
        copies.append(
            pltpu.make_async_copy(source, out.at[:, pl.ds(0, CHIP)], sems.at[step])
        )
    for copy in copies:
        copy.start()
    copies[0].wait()
    left, right = held[0:1, :], held[1:2, :]
    slot = lax.broadcasted_iota(jnp.int32, left.shape, 1)
    live = jnp.where(slot < count[0], left * 24 + (right - left), -1).astype(f32)
    for copy in copies[1:]:
        copy.wait()
    for out in outs:
        out[:, CHIP:] = jnp.full((4, 128), -1.0, f32)
        out[0:1, CHIP : CHIP + live.shape[1]] = live


def split(place, count, pairs, innovations):
    part = jax.ShapeDtypeStruct((4, WIDE), f32)
    return pl.pallas_call(
        split_kernel,
        out_shape=(part, part, part, part),
        in_specs=smem(2) + hbm(2),
        out_specs=vmem(4),
        scratch_shapes=[
            pltpu.VMEM(pairs.shape, jnp.int32),
            pltpu.SemaphoreType.DMA((5,)),
        ],
        compiler_params=params(4),
        name="split",
    )(place, count, in_hbm(pairs), in_hbm(innovations))


def assemble_kernel(place, own, behind1, behind2, behind3, out):
    for y in range(4):
        step = (place[2] - y) & 3
        value = jnp.where(step == 0, own[...], behind1[...])
        value = jnp.where(step == 2, behind2[...], value)
        value = jnp.where(step == 3, behind3[...], value)
        out[4 * y : 4 * y + 4, :] = value


def assemble(place, own, behind1, behind2, behind3):
    return pl.pallas_call(
        assemble_kernel,
        out_shape=jax.ShapeDtypeStruct((16, WIDE), f32),
        in_specs=smem(1) + vmem(4),
        out_specs=vmem(1)[0],
        compiler_params=params(4),
        name="assemble",
    )(place, own, behind1, behind2, behind3)


def pair_flags(row_at, core, mine, other):
    sub = lax.broadcasted_iota(jnp.int32, (8, 128), 0)
    col = lax.broadcasted_iota(jnp.int32, (8, 128), 1)
    far = col < 24
    near = col - lax.div(col, 8) * 8
    ahead = 8 * (lax.div(col, 8) + 1)
    offset = jnp.where(far, ahead + sub - near, jnp.abs(near - sub))
    left_up = jnp.where(far, near, jnp.minimum(near, sub))
    left_down = jnp.where(far, 7 - sub, 7 - jnp.maximum(near, sub))
    left = jnp.where(core == 0, left_up, left_down)
    valid = (offset >= 0) & (offset <= KMAX) & (col < 32)
    target = jnp.where(valid, (row_at * 8 + left) * 24 + offset, -7).astype(f32)
    hit = jnp.zeros((8, 128), f32)
    for source in (mine, other):
        known = source[0:1, CHIP:]
        for y in (1, 2, 3):
            known = jnp.where(row_at == y, source[4 * y : 4 * y + 1, CHIP:], known)
        for i in range(96):
            code = jnp.broadcast_to(known[0:1, i : i + 1], (8, 128))
            hit = jnp.where(code == target, 1.0, hit)
    return jnp.where(hit > 0.5, 0.0, FAR)


def points_kernel(
    place,
    all_counts,
    all_coords,
    all_std,
    all_variance,
    base,
    aux,
    first,
    right,
    coords,
    std,
    variance,
    counts,
    sems,
):
    row_at, core = place[0], place[1]
    chip = pl.ds(pl.multiple_of(row_at * CHIP, CHIP), CHIP)
    copies = [
        pltpu.make_async_copy(source.at[:, chip], to, sems.at[i])
        for i, (source, to) in enumerate(
            ((all_coords, coords), (all_std, std), (all_variance, variance))
        )
    ]
    copies.append(pltpu.make_async_copy(all_counts, counts, sems.at[3]))
    for copy in copies:
        copy.start()
    base[...] = jnp.zeros((8, CHIP), f32)
    for copy in copies:
        copy.wait()
    lane = lax.broadcasted_iota(jnp.int32, (1, BLOCK), 1)
    for j in range(8):
        source = j + core * (7 - 2 * j)
        here = slice(j * BLOCK, (j + 1) * BLOCK)
        region = pl.ds(pl.multiple_of(source * BLOCK, BLOCK), BLOCK)
        live = (lane < counts[row_at * 8 + source]).astype(f32)
        base[0:3, here] = coords[:, region]
        aux[0:1, here] = std[0:1, region] * live
        aux[1:2, here] = variance[0:1, region]
    sub = lax.broadcasted_iota(jnp.int32, (8, CHIP), 0)
    points = base[...]
    side = jnp.where(sub < 3, points * (-GAMMA), jnp.where(sub == 3, GAMMA, 0.0))
    a1, a2, a3 = three_parts(side)
    first[...] = a1
    right[0:16, :] = jnp.concatenate([a2, a2], 0).astype(bf16)
    right[16:32, :] = jnp.concatenate([a1, a3], 0).astype(bf16)


def points(place, counts, coords, std, variance):
    return pl.pallas_call(
        points_kernel,
        out_shape=(
            jax.ShapeDtypeStruct((8, CHIP), f32),
            jax.ShapeDtypeStruct((8, CHIP), f32),
            jax.ShapeDtypeStruct((8, CHIP), f32),
            jax.ShapeDtypeStruct((32, CHIP), bf16),
        ),
        in_specs=smem(1) + hbm(4),
        out_specs=vmem(4),
        scratch_shapes=[
            pltpu.VMEM((3, CHIP), f32),
            pltpu.VMEM((1, CHIP), f32),
            pltpu.VMEM((1, CHIP), f32),
            pltpu.SMEM(counts.shape, jnp.int32),
            pltpu.SemaphoreType.DMA((4,)),
        ],
        compiler_params=params(4),
        name="points",
    )(place, in_hbm(counts), in_hbm(coords), in_hbm(std), in_hbm(variance))


def vectors_kernel(place, mine, other, base, aux, halo, vector, flags):
    core = place[1]
    pairs = pair_flags(place[0], core, mine, other)
    flags[...] = pairs
    halo[32:40, 0:CHIP] = base[...]
    halo[32:40, CHIP:] = pairs
    halo[0:32, CHIP:] = jnp.zeros((32, 128), f32)
    for j in range(8):
        here = slice(j * BLOCK, (j + 1) * BLOCK)
        source = (j + core * (7 - 2 * j)) * BLOCK
        local = pl.ds(pl.multiple_of(source, BLOCK), BLOCK)
        spread = aux[0:1, here]
        got, had = other[:, local], mine[:, local]
        for y in range(4):
            rows = slice(4 * y, 4 * y + 4)
            up = jnp.concatenate([had[rows], got[rows]], 0)
            down = jnp.concatenate([got[rows], had[rows]], 0)
            value = jnp.where(core == 0, up, down)
            vector[8 * y : 8 * y + 8, here] = value
            halo[8 * y : 8 * y + 8, here] = value * spread


def vectors(place, mine, other, base, aux):
    return pl.pallas_call(
        vectors_kernel,
        out_shape=(
            jax.ShapeDtypeStruct((40, WIDE), f32),
            jax.ShapeDtypeStruct((ROWS, CHIP), f32),
            jax.ShapeDtypeStruct((8, 128), f32),
        ),
        in_specs=smem(1) + vmem(4),
        out_specs=vmem(3),
        compiler_params=params(4),
        name="vectors",
    )(place, mine, other, base, aux)


def distance(left, right):
    return jnp.maximum(dot(left, right), 1e-30)


def covariance(x):
    z = jnp.maximum(STRETCH - pl.reciprocal(lax.rsqrt(x), approx=True), 0.0)
    z2 = z * z
    return z2 * z2 * (TOP - z)


def times(parts, tile):
    th, tl = two_parts(tile)
    pair = dot(jnp.concatenate(parts, 0), th)
    return (pair[0:ROWS] + pair[ROWS:]) + dot(parts[0], tl)


def sides(count, offset, place, own, halo, first, mask, left, top):
    column = 24 if offset == 0 else 8 * (offset - 1)
    flags = jnp.where(place[1] == 0, own[...], halo[32:40, CHIP:])
    for a in range(8):
        mask[:, a * BLOCK : (a + 1) * BLOCK] = jnp.broadcast_to(
            flags[:, column + a : column + a + 1], (8, BLOCK)
        )
    width = count * BLOCK
    sub = lax.broadcasted_iota(jnp.int32, (8, width), 0)
    points = halo[32:40, 0:width]
    b1, b2, b3 = three_parts(
        jnp.where(sub < 3, points, jnp.where(sub < 5, 1.0, 0.0))
    )
    left[0:width, :] = jnp.concatenate([b1, b2, b1, b2, b3, b1], 0).T.astype(bf16)
    sub = lax.broadcasted_iota(jnp.int32, (8, CHIP), 0)
    a1 = first[...]
    for b in range(count):
        row = jnp.broadcast_to(mask[b : b + 1, :], (8, CHIP))
        top[16 * b : 16 * b + 16, :] = jnp.concatenate(
            [jnp.where(sub == 4, row, a1), a1], 0
        ).astype(bf16)


def side_scratch(count):
    return [
        pltpu.VMEM((8, CHIP), f32),
        pltpu.VMEM((count * BLOCK, 48), bf16),
        pltpu.VMEM((count * 16, CHIP), bf16),
        pltpu.VMEM((2, BLOCK, BLOCK), f32),
    ]


def make_tiles(jobs, left, top, right, kept, held, total):
    def start(n):
        block, here, _, _, _ = jobs[n]
        rows = pl.ds(pl.multiple_of(block * BLOCK, BLOCK), BLOCK)
        upper = pl.ds(pl.multiple_of(block * 16, 16), 16)
        side = jnp.concatenate([top[upper, here], right[:, here]], 0)
        held[n % 2] = distance(left[rows, :], side)

    start(0)
    for n, (_, here, rows, columns, parts) in enumerate(jobs):
        if n + 1 < len(jobs):
            start(n + 1)
        kept[rows, columns] = covariance(held[n % 2])
        total[:, here] += times(parts, kept[rows, columns])


def tiles0_kernel(
    place, own, halo, first, right, kept, total, mask, left, top, held
):
    sides(4, 0, place, own, halo, first, mask, left, top)
    total[...] = jnp.zeros_like(total)
    jobs = []
    for b in range(4):
        rows = slice(b * BLOCK, (b + 1) * BLOCK)
        parts = two_parts(halo[0:ROWS, rows])
        for a in range(8):
            here = slice(a * BLOCK, (a + 1) * BLOCK)
            jobs.append((b, here, rows, here, parts))
    make_tiles(jobs, left, top, right, kept, held, total)


def tiles0(place, own, halo, first, right):
    return pl.pallas_call(
        tiles0_kernel,
        out_shape=(
            pltpu.VMEM((HALF, CHIP), f32),
            jax.ShapeDtypeStruct((ROWS, CHIP), f32),
        ),
        in_specs=smem(1) + vmem(4),
        out_specs=vmem(2),
        scratch_shapes=side_scratch(4),
        compiler_params=params(3),
        name="tiles0",
    )(place, own, halo, first, right)


def tiles_kernel(
    offset,
    place,
    own,
    halo,
    first,
    right,
    before,
    kept,
    total,
    mask,
    left,
    top,
    held,
):
    sides(8, offset, place, own, halo, first, mask, left, top)
    total[...] = before[...]

    def four_blocks(i, carry):
        jobs = []
        for n in range(4):
            b = 4 * i + n
            rows = pl.ds(pl.multiple_of(b * BLOCK, BLOCK), BLOCK)
            parts = two_parts(halo[0:ROWS, rows])
            for a in range(8):
                here = slice(a * BLOCK, (a + 1) * BLOCK)
                jobs.append((b, here, rows, here, parts))
        make_tiles(jobs, left, top, right, kept, held, total)
        return carry

    lax.fori_loop(0, 2, four_blocks, 0)


def tiles(offset, place, own, halo, first, right, before):
    return pl.pallas_call(
        functools.partial(tiles_kernel, offset),
        out_shape=(
            pltpu.VMEM((CHIP, CHIP), f32),
            jax.ShapeDtypeStruct((ROWS, CHIP), f32),
        ),
        in_specs=smem(1) + vmem(5),
        out_specs=vmem(2),
        scratch_shapes=side_scratch(8),
        compiler_params=params(4),
        name=f"tiles{offset}",
    )(place, own, halo, first, right, before)


def edge_kernel(
    place, own, halo, first, right, before, kept, total, mask, left, top, held
):
    sides(7, 3, place, own, halo, first, mask, left, top)
    total[...] = before[...]
    jobs = []
    for j in range(7):
        rows = slice(j * BLOCK, (j + 1) * BLOCK)
        parts = two_parts(halo[0:ROWS, rows])
        for a in range(j + 1, 8):
            here = slice(a * BLOCK, (a + 1) * BLOCK)
            at = (a * (a - 1) // 2 + j) * BLOCK
            jobs.append((j, here, slice(at, at + BLOCK), slice(0, BLOCK), parts))
    make_tiles(jobs, left, top, right, kept, held, total)


def edge_tiles(place, own, halo, first, right, before):
    return pl.pallas_call(
        edge_kernel,
        out_shape=(
            pltpu.VMEM((28 * BLOCK, BLOCK), f32),
            jax.ShapeDtypeStruct((ROWS, CHIP), f32),
        ),
        in_specs=smem(1) + vmem(5),
        out_specs=vmem(2),
        scratch_shapes=side_scratch(7),
        compiler_params=params(4),
        name="tiles3",
    )(place, own, halo, first, right, before)


def apply_kernel(depth, vector, kept, before, total):
    uh, ul = two_parts(vector[0:ROWS, 0:depth])
    for n in range(0, CHIP, BLOCK):
        here = slice(n, n + BLOCK)
        value = before[:, here]
        for k in range(0, depth, BLOCK):
            rows = slice(k, k + BLOCK)
            value = value + times((uh[:, rows], ul[:, rows]), kept[rows, here])
        total[:, here] = value


def apply(vector, kept, before):
    return pl.pallas_call(
        functools.partial(apply_kernel, kept.shape[0]),
        out_shape=jax.ShapeDtypeStruct((ROWS, CHIP), f32),
        in_specs=vmem(3),
        out_specs=vmem(1)[0],
        compiler_params=params(3),
        name="apply",
    )(vector, kept, before)


def edge_apply_kernel(vector, kept, before, total):
    uh, ul = two_parts(vector[0:ROWS, 0 : 7 * BLOCK])
    total[:, 0:BLOCK] = before[:, 0:BLOCK]
    for a in range(1, 8):
        here = slice(a * BLOCK, (a + 1) * BLOCK)
        value = before[:, here]
        for j in range(a):
            rows = slice(j * BLOCK, (j + 1) * BLOCK)
            at = (a * (a - 1) // 2 + j) * BLOCK
            parts = (uh[:, rows], ul[:, rows])
            value = value + times(parts, kept[at : at + BLOCK, :])
        total[:, here] = value


def edge_apply(vector, kept, before):
    return pl.pallas_call(
        edge_apply_kernel,
        out_shape=jax.ShapeDtypeStruct((ROWS, CHIP), f32),
        in_specs=vmem(3),
        out_specs=vmem(1)[0],
        compiler_params=params(3),
        name="apply3",
    )(vector, kept, before)


def combine_kernel(mine, other, aux, vector, image, scaled):
    for j in range(8):
        here = slice(j * BLOCK, (j + 1) * BLOCK)
        there = slice((7 - j) * BLOCK, (8 - j) * BLOCK)
        spread = aux[0:1, here]
        value = (mine[:, here] + other[:, there]) * spread
        value = value + aux[1:2, here] * vector[:, here]
        image[:, here] = value
        scaled[:, here] = value * spread


def combine(mine, other, aux, vector):
    shape = jax.ShapeDtypeStruct((ROWS, CHIP), f32)
    return pl.pallas_call(
        combine_kernel,
        out_shape=(shape, shape),
        in_specs=vmem(4),
        out_specs=vmem(2),
        compiler_params=params(3),
        name="combine",
    )(mine, other, aux, vector)


def finish_kernel(
    place, mine, other, aux, vector, image, own, ahead1, ahead2, ahead3, last, packed
):
    row_at, core = place[2], place[1]
    sums = [jnp.zeros((ROWS, 1), f32) for _ in range(4)]
    for j in range(8):
        here = slice(j * BLOCK, (j + 1) * BLOCK)
        there = slice((7 - j) * BLOCK, (8 - j) * BLOCK)
        start, first = vector[:, here], image[:, here]
        value = (mine[:, here] + other[:, there]) * aux[0:1, here]
        value = value + aux[1:2, here] * first
        last[:, here] = value
        terms = (start * start, start * first, first * first, first * value)
        sums = [s + jnp.sum(t, axis=1, keepdims=True) for s, t in zip(sums, terms)]
    lane = lax.broadcasted_iota(jnp.int32, (ROWS, 128), 1)
    row = jnp.zeros((ROWS, 128), f32)
    for i in range(4):
        row = jnp.where(lane == i, sums[i], row)
    packed[...] = row
    for step, out in enumerate((own, ahead1, ahead2, ahead3)):
        rows = pl.ds(pl.multiple_of(lax.rem(row_at + step, 4) * 8, 8), 8)

        def chosen(value):
            return jnp.where(core == 0, value[0:4], value[4:8])

        for j in range(8):
            here = slice(j * BLOCK, (j + 1) * BLOCK)
            to = (j + core * (7 - 2 * j)) * BLOCK
            out[:, pl.ds(pl.multiple_of(to, BLOCK), BLOCK)] = chosen(image[rows, here])
            out[:, pl.ds(pl.multiple_of(CHIP + to, BLOCK), BLOCK)] = chosen(
                last[rows, here]
            )
        out[:, 2 * CHIP :] = chosen(packed[rows, :])


def finish(place, mine, other, aux, vector, image):
    part = jax.ShapeDtypeStruct((4, 2 * CHIP + 128), f32)
    return pl.pallas_call(
        finish_kernel,
        out_shape=(part, part, part, part),
        in_specs=smem(1) + vmem(5),
        out_specs=vmem(4),
        scratch_shapes=[pltpu.VMEM((ROWS, CHIP), f32), pltpu.VMEM((ROWS, 128), f32)],
        compiler_params=params(4),
        name="finish",
    )(place, mine, other, aux, vector, image)


def region_sums_kernel(own, behind1, behind2, behind3, out):
    total = own[:, 2 * CHIP :] + behind1[:, 2 * CHIP :]
    total = total + (behind2[:, 2 * CHIP :] + behind3[:, 2 * CHIP :])
    out[...] = jnp.broadcast_to(total[None], out.shape)


def region_sums(regions, parts):
    return pl.pallas_call(
        region_sums_kernel,
        out_shape=jax.ShapeDtypeStruct((regions, 4, 128), f32),
        in_specs=vmem(4),
        out_specs=vmem(1)[0],
        compiler_params=params(4),
        name="region_sums",
    )(*parts)


def result_kernel(
    place, sums, innovations, own, behind1, behind2, behind3, field, residual
):
    totals = jnp.sum(sums[...], axis=0)
    bb, bk, kk, kl = (totals[:, i : i + 1] for i in range(4))
    alpha = bb / bk
    norm = alpha * alpha * kk - 2.0 * alpha * bk + bb
    grown = 1.0 + norm / bb
    energy = grown * grown * bk - 2.0 * alpha * grown * kk + alpha * alpha * kl
    step = norm / energy
    for back, part in enumerate((own, behind1, behind2, behind3)):
        at = chip_at(place, (place[2] - back) & 3) * CHIP
        here = pl.ds(pl.multiple_of(at, CHIP), CHIP)
        start = innovations[:, here]
        first, last = part[:, 0:CHIP], part[:, CHIP : 2 * CHIP]
        field[:, here] = alpha * start + step * (grown * start - alpha * first)
        residual[:, here] = (
            start - alpha * first - step * (grown * first - alpha * last)
        )


def result(place, sums, innovations, parts):
    shape = jax.ShapeDtypeStruct(innovations.shape, f32)
    return pl.pallas_call(
        result_kernel,
        out_shape=(shape, shape),
        in_specs=smem(1) + vmem(6),
        out_specs=vmem(2),
        compiler_params=params(4),
        name="result",
    )(place, sums, innovations, *parts)


def device(chip, core):
    region, place = divmod(chip, 4)
    return 8 * region + 2 * (place ^ (place >> 1) ^ (2 * (region % 2))) + core


def neighbours(block, step, chips):
    route = []
    for m in range(chips - step):
        route.append((device(m + step, 0), device(m, 0)))
        route.append((device(m, 1), device(m + step, 1)))
    return lax.ppermute(block, AXES, route)


def sibling(block, chips):
    route = [(i, i ^ 1) for i in range(2 * chips)]
    return lax.ppermute(block, AXES, route)


after = lax.optimization_barrier


def along_y(parts):
    columns = lax.axis_size("cols")
    return [
        lax.ppermute(
            part, "cols", [(i, (i + 2 * step) % columns) for i in range(columns)]
        )
        for step, part in enumerate(parts, 1)
    ]


def per_device(
    innovations, coords, background_std, obs_variance, block_count, pair_list, pair_count
):
    regions = lax.axis_size("region")
    chips = regions * lax.axis_size("cols") // 2
    column = lax.axis_index("cols")
    row_at = column // 2
    odd = lax.axis_index("region") % 2
    turned = row_at ^ (2 * odd)
    place = jnp.stack([turned ^ (turned >> 1), column % 2, row_at, odd])

    own, *ahead = split(place, pair_count, pair_list, innovations)
    behind = along_y(ahead)
    base, aux, first, right = points(
        place,
        block_count,
        coords,
        background_std.reshape(1, -1),
        obs_variance.reshape(1, -1),
    )
    behind, base, aux = after((behind, base, aux))
    half = assemble(place, own, *behind)
    halo, vector, flags = vectors(place, half, sibling(half, chips), base, aux)

    halos = [neighbours(halo, step, chips) for step in (1, 2, 3)]
    made, total = tiles0(place, flags, halo, first, right)
    kept = [made]
    for k in (1, 2):
        made, total = tiles(k, place, flags, halos[k - 1], first, right, total)
        kept.append(made)
    made, part = edge_tiles(place, flags, halos[2], first, right, total)
    kept.append(made)
    image, scaled = combine(part, sibling(part, chips), aux, vector)

    halos = [scaled] + [neighbours(scaled, step, chips) for step in (1, 2, 3)]
    total = jnp.zeros((ROWS, CHIP), f32)
    for k in range(3):
        total = apply(halos[k], kept[k], total)
    part = edge_apply(halos[3], kept[3], total)
    own, *ahead = finish(place, part, sibling(part, chips), aux, vector, image)

    parts = [own] + along_y(ahead)
    sums = lax.all_to_all(region_sums(regions, parts), "region", 0, 0, tiled=True)
    return result(place, sums, innovations, parts)


def solution(mesh):
    placed = (
        P("cols", "region"),
        P(None, "region"),
        P("region"),
        P("region"),
        P("region"),
        P(None, ("region", "cols")),
        P(("region", "cols")),
    )
    return jax.shard_map(
        per_device,
        mesh=mesh,
        in_specs=placed,
        out_specs=(P("cols", "region"), P("cols", "region")),
        check_vma=False,
    )
```
